128 devices in a mesh: row: 8 (over z, x_lo), col: 16 (over x_hi, y, core).
Axes of the slice: x: 4 (x_hi: 2, x_lo: 2; x = x_hi * 2 + x_lo), y: 4, z: 4, core: 2. Of those that a mesh axis runs over, the one named last changes fastest.
Arguments:
- points_gen: bfloat16 [24576, 128], P(('row', 'col')), may hold values from -6 to 6
- points_obs: bfloat16 [16384, 128], P(('col', 'row')), may hold values from -6 to 6
- log_mass_gen: float32 [24576], P('row'), may hold values from -1 to 1
- log_mass_obs: float32 [16384], P('col'), may hold values from -1 to 1
Outputs:
- potential_gen: float32 [24576], P('row')
- potential_obs: float32 [16384], P('col')
- costate: float32 [24576, 128], P(('row', 'col'))
The draws below stay inside these ranges and needn't reach their ends.
All inputs are finite; a program needn't handle non-finite values.
Results may differ from the reference program's by a relative error of at most 0.0015.
Values may be sent and summed in bfloat16 or wider, within the bound.
No kernel may reach another device: no remote copies, remote signals or barrier semaphores. Data moves between devices by JAX's collectives and lax.ppermute only.
A program may use at most 64 MiB of HBM per device.

```python
import jax
import jax.numpy as jnp

DIM = 128
ITERS = 4
NG = 24576
NO = 16384


def block_scale(key, shape, split, low, high):
    def one(dim, blocks):
        steps = jax.random.uniform(jax.random.fold_in(jax.random.fold_in(key, 6), dim), (blocks,), jnp.float32, low / len(split), high / len(split))
        return jnp.repeat(jnp.exp(steps), shape[dim] // blocks).reshape((-1,) + (1,) * (len(shape) - dim - 1))

    loudness = one(*split[0])
    for cut in split[1:]:
        loudness = loudness * one(*cut)
    return loudness


def bell_draw(key, extent, scale, reach, shards=(), dtype=jnp.bfloat16):
    values = jax.random.normal(key, extent, jnp.float32) * scale
    if len(shards) > 0:
        values = block_scale(key, extent, shards, -0.22, 0.18) * values
    return jnp.clip(values, min=-reach, max=reach).astype(dtype)


def setup_inputs(seed: int = 0) -> dict:
    arg_keys = jax.random.split(jax.random.key(seed), 5)
    return {
        "points_gen": bell_draw(arg_keys[0], (NG, DIM), 1.0, 6.0, ((0, 128),)),
        "points_obs": bell_draw(arg_keys[1], (NO, DIM), 1.0, 6.0, ((0, 128),)),
        "log_mass_gen": jnp.clip(jax.random.uniform(arg_keys[2], (NG,), jnp.float32, -1.0, 1.0) * block_scale(arg_keys[2], (NG,), ((0, 8),), -0.4, 0.0), -1.0, 1.0),
        "log_mass_obs": jnp.clip(jax.random.uniform(arg_keys[3], (NO,), jnp.float32, -1.0, 1.0) * block_scale(arg_keys[3], (NO,), ((0, 16),), -0.4, 0.0), -1.0, 1.0),
    }


def reference(points_gen, points_obs, log_mass_gen, log_mass_obs):
    temper = points_gen.shape[1] / 64.0
    gen_wide = points_gen.astype(jnp.float32)
    obs_wide = points_obs.astype(jnp.float32)
    gen_sq = jnp.sum(gen_wide * gen_wide, axis=1)
    obs_sq = jnp.sum(obs_wide * obs_wide, axis=1)
    inner_prod = jnp.dot(points_gen, points_obs.T, preferred_element_type=jnp.float32)
    cost_tile = gen_sq[:, None] + obs_sq[None, :] - 2.0 * inner_prod
    potential_gen = jnp.zeros(log_mass_gen.shape, jnp.float32)
    potential_obs = jnp.zeros(log_mass_obs.shape, jnp.float32)
    row_scores = None
    top = None
    total = None
    for step in range(ITERS):
        col_scores = log_mass_gen[:, None] + (potential_gen[:, None] - cost_tile) / temper
        col_top = jnp.max(col_scores, axis=0)
        col_total = jnp.sum(jnp.exp(col_scores - col_top[None, :]), axis=0)
        potential_obs = temper * (log_mass_obs - col_top - jnp.log(col_total))
        row_scores = log_mass_obs[None, :] + (potential_obs[None, :] - cost_tile) / temper
        top = jnp.max(row_scores, axis=1)
        total = jnp.sum(jnp.exp(row_scores - top[:, None]), axis=1)
        potential_gen = temper * (log_mass_gen - top - jnp.log(total))
    weights = jnp.exp(row_scores - top[:, None]).astype(jnp.bfloat16)
    numerator = jnp.dot(weights, points_obs, preferred_element_type=jnp.float32)
    costate = gen_wide - numerator / total[:, None]
    return potential_gen, potential_obs, costate
```

```python
import functools
import math

import jax
import jax.numpy as jnp
from jax import lax
from jax.experimental import pallas as pl
from jax.experimental.pallas import tpu as pltpu
from jax.sharding import PartitionSpec as P

ITERS = 4
LANES = 128
CHUNK = 256
SAMPLE = 256
LOW, HIGH = 1e-20, 1e30
STEEP, FAINT, NOTHING = 20.0, 60.0, 60.0
VMEM = pl.BlockSpec(memory_space=pltpu.VMEM)
SMEM = pl.BlockSpec(memory_space=pltpu.SMEM)
NT = (((1,), (1,)), ((), ()))


def lse_over(parts):
    top = functools.reduce(jnp.maximum, parts)
    return top + jnp.log(sum(jnp.exp(part - top) for part in parts))


def planes(ref):
    return [ref[k] for k in range(ref.shape[0])]


def scores(left, right, left_wide):
    prod = lax.dot_general(left, right, NT, preferred_element_type=jnp.float32)
    return prod + jnp.concatenate([left_wide] * (right.shape[0] // LANES), axis=1)


def fold(values, op):
    rows, width = values.shape
    return op(values.reshape(rows // 8, 8, width), axis=0)


def store_row(ref, first, row):
    for part in range(row.shape[1] // LANES):
        ref[pl.ds(first + part, 1), :] = row[:, part * LANES : (part + 1) * LANES]


def dense_of(row):
    return jnp.concatenate([row[:, k * LANES : (k + 1) * LANES] for k in range(row.shape[1] // LANES)], axis=0)


def row_of(dense):
    return jnp.concatenate([dense[k : k + 1, :] for k in range(dense.shape[0])], axis=1)


def widen(dense, wide_ref):
    for part in range(dense.shape[0]):
        row = jnp.broadcast_to(dense[part : part + 1, :], (LANES, LANES))
        wide_ref[part * LANES : (part + 1) * LANES, :] = jnp.transpose(row)


def squares(points):
    wide = points.astype(jnp.float32)
    square = wide * wide
    high = square.astype(jnp.bfloat16)
    low = (square - high.astype(jnp.float32)).astype(jnp.bfloat16)
    ones = jnp.ones((8, LANES), jnp.bfloat16)
    row = lax.dot_general(ones, high, NT, preferred_element_type=jnp.float32)
    row += lax.dot_general(ones, low, NT, preferred_element_type=jnp.float32)
    return dense_of(row[:1, :])


def in_parts(row):
    high = row.astype(jnp.bfloat16).astype(jnp.float32)
    middle = (row - high).astype(jnp.bfloat16).astype(jnp.float32)
    low = row - high - middle
    line = lax.broadcasted_iota(jnp.int32, (16, row.shape[1]), 0)
    parts = jnp.where(line == 0, high, jnp.where(line == 1, middle, jnp.where(line == 2, low, 0.0)))
    return parts.astype(jnp.bfloat16)


def means_of(left_ref, chunk, values, mean_ref):
    left_t = jnp.transpose(left_ref[...].astype(jnp.float32))
    left_t = jnp.concatenate([left_t, jnp.ones((16, left_t.shape[1]), jnp.float32)], axis=0).astype(jnp.bfloat16)
    numer = jnp.dot(left_t, values.astype(jnp.bfloat16), preferred_element_type=jnp.float32)
    mean = numer[:LANES, :] / numer[LANES : LANES + 1, :]
    mean_ref[pl.ds(pl.multiple_of(chunk * CHUNK, CHUNK), CHUNK), :] = jnp.transpose(mean)


def exact_pass(left_ref, right_ref, wide_ref, shift_ref, total_ref, mean_ref=None):
    n, m = left_ref.shape[0], right_ref.shape[0]
    block = 512
    per = CHUNK // LANES

    def one(chunk, carry):
        right = right_ref[pl.ds(pl.multiple_of(chunk * CHUNK, CHUNK), CHUNK), :]

        def largest(step, top):
            rows = pl.ds(pl.multiple_of(step * block, block), block)
            return jnp.maximum(top, fold(scores(left_ref[rows, :], right, wide_ref[rows, :]), jnp.max))

        top = lax.fori_loop(0, n // block, largest, jnp.full((8, CHUNK), -3e38, jnp.float32))
        top = jnp.max(top, axis=0, keepdims=True)

        def add(step, total):
            rows = pl.ds(pl.multiple_of(step * block, block), block)
            return total + fold(jnp.exp(scores(left_ref[rows, :], right, wide_ref[rows, :]) - top), jnp.sum)

        total = lax.fori_loop(0, n // block, add, jnp.zeros((8, CHUNK), jnp.float32))
        store_row(shift_ref, chunk * per, top)
        store_row(total_ref, chunk * per, jnp.sum(total, axis=0, keepdims=True))
        if mean_ref is not None:
            means_of(left_ref, chunk, jnp.exp(scores(left_ref[...], right, wide_ref[...]) - top), mean_ref)
        return carry

    lax.fori_loop(0, m // CHUNK, one, 0)


def sampled_pass(left_ref, right_ref, wide_ref, shift_ref, total_ref, matrix_ref=None):
    m = right_ref.shape[0]
    per = CHUNK // LANES
    for chunk in range(m // CHUNK):
        right = right_ref[chunk * CHUNK : (chunk + 1) * CHUNK, :]
        some = scores(left_ref[:SAMPLE, :], right, wide_ref[:SAMPLE, :])
        shift = jnp.max(fold(some, jnp.max), axis=0, keepdims=True)
        values = jnp.exp(scores(left_ref[...], right, wide_ref[...]) - shift)
        total = jnp.sum(fold(values, jnp.sum), axis=0, keepdims=True)
        store_row(shift_ref, chunk * per, shift)
        store_row(total_ref, chunk * per, total)
        if matrix_ref is not None:
            matrix_ref[:, chunk * CHUNK : (chunk + 1) * CHUNK] = values.astype(jnp.bfloat16)

    @pl.when(jnp.logical_not(jnp.max(total_ref[...]) < HIGH))
    def _():
        exact_pass(left_ref, right_ref, wide_ref, shift_ref, total_ref)
        if matrix_ref is not None:
            for chunk in range(m // CHUNK):
                across = pl.ds(chunk * CHUNK, CHUNK)
                top = row_of(shift_ref[chunk * per : (chunk + 1) * per, :])
                values = jnp.exp(scores(left_ref[...], right_ref[across, :], wide_ref[...]) - top)
                matrix_ref[:, across] = values.astype(jnp.bfloat16)

    return shift_ref[...] + jnp.log(total_ref[...])


def spread(out_ref, value):
    for copy in range(out_ref.shape[0]):
        out_ref[copy] = value


def first_kernel(
    core_ref, same_ref, other_ref, right_ref, mass_ref,
    out_ref, left_ref, sq_ref, right_sq_ref, wide_ref, shift_ref, total_ref,
):
    core = core_ref[0]
    right_sq_ref[...] = squares(right_ref[...])
    count, own, _ = same_ref.shape
    for k in range(count):
        left_ref[pl.ds(pl.multiple_of((2 * k + core) * own, 64), own), :] = same_ref[k]
        left_ref[pl.ds(pl.multiple_of((2 * k + 1 - core) * own, 64), own), :] = other_ref[k]
    sq_ref[...] = squares(left_ref[...])
    widen(mass_ref[...] - 0.5 * sq_ref[...], wide_ref)
    spread(out_ref, sampled_pass(left_ref, right_ref, wide_ref, shift_ref, total_ref))


def second_kernel(
    left_ref, right_ref, mass_ref, from_ref,
    out_ref, left_add_ref, right_add_ref, matrix_ref, wide_ref, shift_ref, total_ref,
):
    offset = 2.0 * mass_ref[...] - lse_over(planes(from_ref))
    left_add_ref[...] = offset
    widen(offset, wide_ref)
    spread(out_ref, sampled_pass(left_ref, right_ref, wide_ref, shift_ref, total_ref, matrix_ref))
    right_add_ref[...] = -shift_ref[...]


def close_pass(left_ref, right_ref, offset, fits, add_ref, wide_ref, shift_ref, total_ref, mean_ref=None):
    shift_ref[...] = -add_ref[...]
    totals = total_ref[...]

    @pl.when(jnp.logical_not(fits & (jnp.min(totals) > LOW) & (jnp.max(totals) < HIGH)))
    def _():
        widen(offset, wide_ref)
        exact_pass(left_ref, right_ref, wide_ref, shift_ref, total_ref, mean_ref)


def col_kernel(
    matrix_ref, obs_ref, gen_ref, mass_ref, from_ref, first_ref, obs_add_ref, gen_add_ref,
    out_ref, wide_ref, shift_ref, total_ref,
):
    offset = 2.0 * mass_ref[...] - lse_over(planes(from_ref))
    gain = offset - gen_add_ref[...]
    level = offset + first_ref[0]
    factors = jnp.exp(gain)
    for block in range(obs_ref.shape[0] // LANES):
        rows = pl.ds(block * LANES, LANES)
        total = jnp.zeros((LANES, LANES), jnp.float32)
        for part in range(gain.shape[0]):
            values = matrix_ref[rows, part * LANES : (part + 1) * LANES].astype(jnp.float32)
            total += values * factors[part : part + 1, :]
        total_ref[block : block + 1, :] = jnp.sum(jnp.transpose(total), axis=0, keepdims=True)
    lost = jnp.max(jnp.where(gain < -FAINT, level, -3e38))
    fits = (jnp.max(level) < STEEP) & (lost < -NOTHING)
    close_pass(gen_ref, obs_ref, offset, fits, obs_add_ref, wide_ref, shift_ref, total_ref)
    spread(out_ref, shift_ref[...] + jnp.log(total_ref[...]))


def row_kernel(
    matrix_ref, obs_ref, gen_ref, mass_ref, from_ref, obs_add_ref, gen_add_ref,
    out_ref, wide_ref, shift_ref, total_ref,
):
    offset = 2.0 * mass_ref[...] - lse_over(planes(from_ref))
    gain = offset - obs_add_ref[...]
    total = jnp.dot(in_parts(row_of(jnp.exp(gain))), matrix_ref[...], preferred_element_type=jnp.float32)
    total_ref[...] = dense_of(jnp.sum(total[:8, :], axis=0, keepdims=True))
    close_pass(obs_ref, gen_ref, offset, mild(gain), gen_add_ref, wide_ref, shift_ref, total_ref)
    spread(out_ref, shift_ref[...] + jnp.log(total_ref[...]))


def mild(gain):
    return (jnp.max(gain) < STEEP) & (jnp.min(gain) > -FAINT)


def mean_kernel(
    core_ref, matrix_ref, left_ref, right_ref, mass_ref, from_ref, left_add_ref, right_add_ref,
    out_ref, keep_ref, send_ref, wide_ref, shift_ref, total_ref, mean_ref,
):
    offset = 2.0 * mass_ref[...] - lse_over(planes(from_ref))
    gain = offset - left_add_ref[...]
    weight = row_of(jnp.exp(gain))
    left_t = jnp.transpose(left_ref[...].astype(jnp.float32)) * weight
    high = left_t.astype(jnp.bfloat16)
    low = (left_t - high.astype(jnp.float32)).astype(jnp.bfloat16)
    factors = jnp.concatenate([high, low, in_parts(weight)], axis=0)
    for chunk in range(right_ref.shape[0] // CHUNK):
        across = pl.ds(chunk * CHUNK, CHUNK)
        sums = jnp.dot(factors, matrix_ref[:, across], preferred_element_type=jnp.float32)
        total = jnp.sum(sums[2 * LANES : 2 * LANES + 8, :], axis=0, keepdims=True)
        store_row(total_ref, chunk * CHUNK // LANES, total)
        mean_ref[across, :] = jnp.transpose((sums[:LANES, :] + sums[LANES : 2 * LANES, :]) / total)
    close_pass(left_ref, right_ref, offset, mild(gain), right_add_ref, wide_ref, shift_ref, total_ref, mean_ref)
    out_ref[...] = shift_ref[...] + jnp.log(total_ref[...])
    core = core_ref[0]
    count, own, _ = keep_ref.shape
    for k in range(count):
        keep_ref[k] = mean_ref[pl.ds(pl.multiple_of((2 * k + core) * own, 64), own), :]
        send_ref[k] = mean_ref[pl.ds(pl.multiple_of((2 * k + 1 - core) * own, 64), own), :]


def pair_kernel(core_ref, keep_ref, came_ref, lse_ref, came_lse_ref, out_ref, wide_ref):
    core = core_ref[0]
    count, own, _ = keep_ref.shape
    both = lse_over([lse_ref[...], came_lse_ref[...]])
    widen(jnp.exp(lse_ref[...] - both), wide_ref)
    for k in range(count):
        share = wide_ref[pl.ds(pl.multiple_of((2 * k + core) * own, 64), own), :]
        out_ref[k, :own, :] = came_ref[k] + share * (keep_ref[k] - came_ref[k])
        out_ref[k, own:, :] = both


def last_kernel(col_ref, all_ref, points_ref, mass_ref, sq_ref, gen_ref, costate_ref, share_ref, wide_ref):
    own = points_ref.shape[0]
    count = all_ref.shape[0]
    parts = [all_ref[k, own:, :] for k in range(count)]
    total = lse_over(parts)
    gen_ref[...] = 2.0 * mass_ref[...] + sq_ref[...] - 2.0 * total
    first = col_ref[0] * own
    line = first // LANES
    inside = pl.multiple_of(first - line * LANES, 64)
    result = points_ref[...].astype(jnp.float32)
    span = wide_ref.shape[1] // LANES
    for k in range(count):
        share_ref[k] = jnp.exp(parts[k] - total)
        for part in range(span):
            row = jnp.broadcast_to(share_ref[k, pl.ds(line + part, 1), :], (LANES, LANES))
            wide_ref[k, part * LANES : (part + 1) * LANES, :] = jnp.transpose(row)
        result -= wide_ref[k, pl.ds(inside, own), :] * all_ref[k, :own, :]
    costate_ref[...] = result


def call(kernel, ins, outs, scratch, flops=0, exps=0):
    moved = sum(math.prod(x.shape) * x.dtype.itemsize for x in list(ins) + list(outs))
    return pl.pallas_call(
        kernel,
        out_shape=outs,
        in_specs=[SMEM if x.dtype == jnp.int32 else VMEM for x in ins],
        out_specs=[VMEM] * len(outs),
        scratch_shapes=scratch,
        compiler_params=pltpu.CompilerParams(vmem_limit_bytes=28 * 2**20),
        cost_estimate=pl.CostEstimate(flops=flops, bytes_accessed=moved, transcendentals=exps),
    )(*ins)


def f32(*shape):
    return jax.ShapeDtypeStruct(shape, jnp.float32)


def wide_scratch(n):
    return pltpu.VMEM((n, LANES), jnp.float32)


def body(n_row, n_col, points_gen, points_obs, log_mass_gen, log_mass_obs):
    own = points_gen.shape[0]
    half = n_col // 2
    groups = [list(range(core, n_col, 2)) for core in range(2)]
    pair = [(k, k ^ 1) for k in range(n_col)]
    col = lax.axis_index("col").astype(jnp.int32)
    core = lax.rem(col, 2).reshape(1)
    n, m = own * n_col, points_obs.shape[0] * n_row
    lines, obs_lines = n // LANES, m // LANES

    def over_row(blocks):
        return lax.all_to_all(blocks, "row", 0, 0)

    def over_col(blocks):
        return lax.all_to_all(blocks, "col", 0, 0)

    def over_chips(blocks):
        return lax.all_to_all(blocks, "col", 0, 0, axis_index_groups=groups)

    same = over_chips(jnp.broadcast_to(points_gen[None], (half,) + points_gen.shape))
    obs = over_row(jnp.broadcast_to(points_obs[None], (n_row,) + points_obs.shape)).reshape(m, LANES)
    other = lax.ppermute(same, "col", pair)
    mass_gen = log_mass_gen.reshape(lines, LANES)
    mass_obs = log_mass_obs.reshape(obs_lines, LANES)

    cost = dict(flops=2 * n * m * LANES, exps=n * m)
    product_cost = dict(flops=2 * n * m * LANES)
    small, gen_small = wide_scratch(obs_lines), wide_scratch(lines)
    col_out, row_out = f32(n_row, obs_lines, LANES), f32(n_col, lines, LANES)
    col_own, gen, gen_sq, obs_sq = call(
        first_kernel,
        (core, same, other, obs, mass_gen),
        [
            col_out,
            jax.ShapeDtypeStruct((n, LANES), points_gen.dtype),
            f32(lines, LANES),
            f32(obs_lines, LANES),
        ],
        [wide_scratch(n), small, small],
        **cost,
    )
    col_all = over_row(col_own)
    row_own, obs_add, gen_add, matrix = call(
        second_kernel,
        (obs, gen, mass_obs, col_all),
        [row_out, f32(obs_lines, LANES), f32(lines, LANES), jax.ShapeDtypeStruct((m, n), jnp.bfloat16)],
        [wide_scratch(m), gen_small, gen_small],
        **cost,
    )
    row_all = over_col(row_own)
    first = row_own
    for step in range(1, ITERS):
        (col_own,) = call(
            col_kernel,
            (matrix, obs, gen, mass_gen, row_all, first, obs_add, gen_add),
            [col_out],
            [wide_scratch(n), small, small],
            **product_cost,
        )
        col_all = over_row(col_own)
        if step == ITERS - 1:
            break
        (row_own,) = call(
            row_kernel,
            (matrix, obs, gen, mass_obs, col_all, obs_add, gen_add),
            [row_out],
            [wide_scratch(m), gen_small, gen_small],
            **product_cost,
        )
        row_all = over_col(row_own)
    row_lse, keep, send = call(
        mean_kernel,
        (core, matrix, obs, gen, mass_obs, col_all, obs_add, gen_add),
        [f32(lines, LANES), f32(half, own, LANES), f32(half, own, LANES)],
        [wide_scratch(m), gen_small, gen_small, wide_scratch(n)],
        **product_cost,
    )
    came = lax.ppermute(send, "col", pair)
    came_lse = lax.ppermute(row_lse, "col", pair)
    (joined,) = call(
        pair_kernel, (core, keep, came, row_lse, came_lse), [f32(half, own + lines, LANES)], [wide_scratch(n)]
    )
    joined_all = over_chips(joined)
    span = own // LANES + 1
    potential_gen, costate = call(
        last_kernel,
        (col.reshape(1), joined_all, points_gen, mass_gen, gen_sq),
        [f32(lines, LANES), f32(own, LANES)],
        [pltpu.VMEM((half, lines, LANES), jnp.float32), pltpu.VMEM((half, span * LANES, LANES), jnp.float32)],
    )
    potential_obs = 2.0 * mass_obs + obs_sq - 2.0 * lse_over([col_all[k] for k in range(n_row)])
    return potential_gen.reshape(-1), potential_obs.reshape(-1), costate


def solution(mesh):
    return jax.shard_map(
        functools.partial(body, mesh.shape["row"], mesh.shape["col"]),
        mesh=mesh,
        in_specs=(P(("row", "col"), None), P(("col", "row"), None), P("row"), P("col")),
        out_specs=(P("row"), P("col"), P(("row", "col"), None)),
        check_vma=False,
    )
```

```python
import functools
import math

import jax
import jax.numpy as jnp
from jax import lax
from jax.experimental import pallas as pl
from jax.experimental.pallas import tpu as pltpu
from jax.sharding import PartitionSpec as P

ITERS = 4
LANES = 128
CHUNK = 256
SAMPLE = 128
LOW, HIGH = 1e-20, 1e30
STEEP, FAINT, NOTHING = 20.0, 60.0, 60.0
VMEM = pl.BlockSpec(memory_space=pltpu.VMEM)
SMEM = pl.BlockSpec(memory_space=pltpu.SMEM)
NT = (((1,), (1,)), ((), ()))


def lse_over(parts):
    top = functools.reduce(jnp.maximum, parts)
    return top + jnp.log(sum(jnp.exp(part - top) for part in parts))


def planes(ref):
    return [ref[k] for k in range(ref.shape[0])]


def scores(left, right, left_wide):
    prod = lax.dot_general(left, right, NT, preferred_element_type=jnp.float32)
    return prod + jnp.concatenate([left_wide] * (right.shape[0] // LANES), axis=1)


def fold(values, op):
    rows, width = values.shape
    return op(values.reshape(rows // 8, 8, width), axis=0)


def store_row(ref, first, row):
    for part in range(row.shape[1] // LANES):
        ref[pl.ds(first + part, 1), :] = row[:, part * LANES : (part + 1) * LANES]


def dense_of(row):
    return jnp.concatenate([row[:, k * LANES : (k + 1) * LANES] for k in range(row.shape[1] // LANES)], axis=0)


def row_of(dense):
    return jnp.concatenate([dense[k : k + 1, :] for k in range(dense.shape[0])], axis=1)


def widen(dense, wide_ref):
    for part in range(dense.shape[0]):
        row = jnp.broadcast_to(dense[part : part + 1, :], (LANES, LANES))
        wide_ref[part * LANES : (part + 1) * LANES, :] = jnp.transpose(row)


def squares(points):
    wide = points.astype(jnp.float32)
    square = wide * wide
    high = square.astype(jnp.bfloat16)
    low = (square - high.astype(jnp.float32)).astype(jnp.bfloat16)
    ones = jnp.ones((8, LANES), jnp.bfloat16)
    row = lax.dot_general(ones, high, NT, preferred_element_type=jnp.float32)
    row += lax.dot_general(ones, low, NT, preferred_element_type=jnp.float32)
    return dense_of(row[:1, :])


def in_parts(row):
    high = row.astype(jnp.bfloat16).astype(jnp.float32)
    middle = (row - high).astype(jnp.bfloat16).astype(jnp.float32)
    low = row - high - middle
    line = lax.broadcasted_iota(jnp.int32, (16, row.shape[1]), 0)
    parts = jnp.where(line == 0, high, jnp.where(line == 1, middle, jnp.where(line == 2, low, 0.0)))
    return parts.astype(jnp.bfloat16)


def means_of(left_ref, chunk, values, mean_ref):
    left_t = jnp.transpose(left_ref[...].astype(jnp.float32))
    left_t = jnp.concatenate([left_t, jnp.ones((16, left_t.shape[1]), jnp.float32)], axis=0).astype(jnp.bfloat16)
    numer = jnp.dot(left_t, values.astype(jnp.bfloat16), preferred_element_type=jnp.float32)
    mean = numer[:LANES, :] / numer[LANES : LANES + 1, :]
    mean_ref[pl.ds(pl.multiple_of(chunk * CHUNK, CHUNK), CHUNK), :] = jnp.transpose(mean)


def exact_pass(left_ref, right_ref, wide_ref, shift_ref, total_ref, mean_ref=None):
    n, m = left_ref.shape[0], right_ref.shape[0]
    block = 512
    per = CHUNK // LANES

    def one(chunk, carry):
        right = right_ref[pl.ds(pl.multiple_of(chunk * CHUNK, CHUNK), CHUNK), :]

        def largest(step, top):
            rows = pl.ds(pl.multiple_of(step * block, block), block)
            return jnp.maximum(top, fold(scores(left_ref[rows, :], right, wide_ref[rows, :]), jnp.max))

        top = lax.fori_loop(0, n // block, largest, jnp.full((8, CHUNK), -3e38, jnp.float32))
        top = jnp.max(top, axis=0, keepdims=True)

        def add(step, total):
            rows = pl.ds(pl.multiple_of(step * block, block), block)
            return total + fold(jnp.exp(scores(left_ref[rows, :], right, wide_ref[rows, :]) - top), jnp.sum)

        total = lax.fori_loop(0, n // block, add, jnp.zeros((8, CHUNK), jnp.float32))
        store_row(shift_ref, chunk * per, top)
        store_row(total_ref, chunk * per, jnp.sum(total, axis=0, keepdims=True))
        if mean_ref is not None:
            means_of(left_ref, chunk, jnp.exp(scores(left_ref[...], right, wide_ref[...]) - top), mean_ref)
        return carry

    lax.fori_loop(0, m // CHUNK, one, 0)


def sampled_pass(left_ref, right_ref, wide_ref, shift_ref, total_ref, matrix_ref=None):
    m = right_ref.shape[0]
    per = CHUNK // LANES
    for chunk in range(m // CHUNK):
        right = right_ref[chunk * CHUNK : (chunk + 1) * CHUNK, :]
        some = scores(left_ref[:SAMPLE, :], right, wide_ref[:SAMPLE, :])
        shift = jnp.max(fold(some, jnp.max), axis=0, keepdims=True)
        values = jnp.exp(scores(left_ref[...], right, wide_ref[...]) - shift)
        total = jnp.sum(fold(values, jnp.sum), axis=0, keepdims=True)
        store_row(shift_ref, chunk * per, shift)
        store_row(total_ref, chunk * per, total)
        if matrix_ref is not None:
            matrix_ref[:, chunk * CHUNK : (chunk + 1) * CHUNK] = values.astype(jnp.bfloat16)

    @pl.when(jnp.logical_not(jnp.max(total_ref[...]) < HIGH))
    def _():
        exact_pass(left_ref, right_ref, wide_ref, shift_ref, total_ref)
        if matrix_ref is not None:
            for chunk in range(m // CHUNK):
                across = pl.ds(chunk * CHUNK, CHUNK)
                top = row_of(shift_ref[chunk * per : (chunk + 1) * per, :])
                values = jnp.exp(scores(left_ref[...], right_ref[across, :], wide_ref[...]) - top)
                matrix_ref[:, across] = values.astype(jnp.bfloat16)

    return shift_ref[...] + jnp.log(total_ref[...])


def spread(out_ref, value):
    for copy in range(out_ref.shape[0]):
        out_ref[copy] = value


def first_kernel(
    core_ref, same_ref, other_ref, right_ref, mass_ref,
    out_ref, left_ref, sq_ref, right_sq_ref, wide_ref, shift_ref, total_ref,
):
    core = core_ref[0]
    right_sq_ref[...] = squares(right_ref[...])
    count, own, _ = same_ref.shape
    for k in range(count):
        left_ref[pl.ds(pl.multiple_of((2 * k + core) * own, 64), own), :] = same_ref[k]
        left_ref[pl.ds(pl.multiple_of((2 * k + 1 - core) * own, 64), own), :] = other_ref[k]
    sq_ref[...] = squares(left_ref[...])
    widen(mass_ref[...] - 0.5 * sq_ref[...], wide_ref)
    spread(out_ref, sampled_pass(left_ref, right_ref, wide_ref, shift_ref, total_ref))


def second_kernel(
    left_ref, right_ref, mass_ref, from_ref,
    out_ref, left_add_ref, right_add_ref, matrix_ref, wide_ref, shift_ref, total_ref,
):
    offset = 2.0 * mass_ref[...] - lse_over(planes(from_ref))
    left_add_ref[...] = offset
    widen(offset, wide_ref)
    spread(out_ref, sampled_pass(left_ref, right_ref, wide_ref, shift_ref, total_ref, matrix_ref))
    right_add_ref[...] = -shift_ref[...]


def close_pass(left_ref, right_ref, offset, bad, add_ref, wide_ref, shift_ref, total_ref, mean_ref=None):
    shift_ref[...] = -add_ref[...]
    totals = total_ref[...]
    fits = (totals > LOW) & (totals < HIGH)
    marks = [jnp.where(mask, 1.0, 0.0) for mask in (bad, jnp.logical_not(fits))]
    flags = [mark[k : k + 8, :] for mark in marks for k in range(0, mark.shape[0], 8)]

    @pl.when(jnp.max(functools.reduce(jnp.maximum, flags)) > 0.0)
    def _():
        widen(offset, wide_ref)
        exact_pass(left_ref, right_ref, wide_ref, shift_ref, total_ref, mean_ref)


def col_kernel(
    matrix_ref, obs_ref, gen_ref, mass_ref, from_ref, first_ref, obs_add_ref, gen_add_ref,
    out_ref, wide_ref, shift_ref, total_ref,
):
    offset = 2.0 * mass_ref[...] - lse_over(planes(from_ref))
    gain = offset - gen_add_ref[...]
    level = offset + first_ref[0]
    factors = jnp.exp(gain)
    for block in range(obs_ref.shape[0] // LANES):
        rows = pl.ds(block * LANES, LANES)
        total = jnp.zeros((LANES, LANES), jnp.float32)
        for part in range(gain.shape[0]):
            values = matrix_ref[rows, part * LANES : (part + 1) * LANES].astype(jnp.float32)
            total += values * factors[part : part + 1, :]
        total_ref[block : block + 1, :] = jnp.sum(jnp.transpose(total), axis=0, keepdims=True)
    bad = (level > STEEP) | ((gain < -FAINT) & (level > -NOTHING))
    close_pass(gen_ref, obs_ref, offset, bad, obs_add_ref, wide_ref, shift_ref, total_ref)
    spread(out_ref, shift_ref[...] + jnp.log(total_ref[...]))


def row_kernel(
    matrix_ref, obs_ref, gen_ref, mass_ref, from_ref, obs_add_ref, gen_add_ref,
    out_ref, wide_ref, shift_ref, total_ref,
):
    offset = 2.0 * mass_ref[...] - lse_over(planes(from_ref))
    gain = offset - obs_add_ref[...]
    total = jnp.dot(in_parts(row_of(jnp.exp(gain))), matrix_ref[...], preferred_element_type=jnp.float32)
    total_ref[...] = dense_of(jnp.sum(total[:8, :], axis=0, keepdims=True))
    close_pass(obs_ref, gen_ref, offset, wild(gain), gen_add_ref, wide_ref, shift_ref, total_ref)
    spread(out_ref, shift_ref[...] + jnp.log(total_ref[...]))


def wild(gain):
    return (gain > STEEP) | (gain < -FAINT)


def mean_kernel(
    core_ref, matrix_ref, left_ref, right_ref, mass_ref, from_ref, left_add_ref, right_add_ref, left_sq_ref,
    potential_ref, out_ref, keep_ref, send_ref, wide_ref, shift_ref, total_ref, mean_ref,
):
    offset = 2.0 * mass_ref[...] - lse_over(planes(from_ref))
    potential_ref[...] = 2.0 * (offset - mass_ref[...]) + left_sq_ref[...]
    gain = offset - left_add_ref[...]
    weight = row_of(jnp.exp(gain))
    left_t = jnp.transpose(left_ref[...].astype(jnp.float32)) * weight
    high = left_t.astype(jnp.bfloat16)
    low = (left_t - high.astype(jnp.float32)).astype(jnp.bfloat16)
    factors = jnp.concatenate([high, low, in_parts(weight)], axis=0)
    for chunk in range(right_ref.shape[0] // CHUNK):
        across = pl.ds(chunk * CHUNK, CHUNK)
        sums = jnp.dot(factors, matrix_ref[:, across], preferred_element_type=jnp.float32)
        total = jnp.sum(sums[2 * LANES : 2 * LANES + 8, :], axis=0, keepdims=True)
        store_row(total_ref, chunk * CHUNK // LANES, total)
        mean_ref[across, :] = jnp.transpose((sums[:LANES, :] + sums[LANES : 2 * LANES, :]) / total)
    close_pass(left_ref, right_ref, offset, wild(gain), right_add_ref, wide_ref, shift_ref, total_ref, mean_ref)
    out_ref[...] = shift_ref[...] + jnp.log(total_ref[...])
    core = core_ref[0]
    count, own, _ = keep_ref.shape
    for k in range(count):
        keep_ref[k] = mean_ref[pl.ds(pl.multiple_of((2 * k + core) * own, 64), own), :]
        send_ref[k] = mean_ref[pl.ds(pl.multiple_of((2 * k + 1 - core) * own, 64), own), :]


def pair_kernel(core_ref, keep_ref, came_ref, lse_ref, came_lse_ref, out_ref, wide_ref):
    core = core_ref[0]
    count, own, _ = keep_ref.shape
    both = lse_over([lse_ref[...], came_lse_ref[...]])
    lines = both.shape[0]
    spaced = both * 8193.0
    high = spaced - (spaced - both)
    low = both - high
    widen(jnp.exp(lse_ref[...] - both), wide_ref)
    for k in range(count):
        share = wide_ref[pl.ds(pl.multiple_of((2 * k + core) * own, 64), own), :]
        out_ref[k, :own, :] = came_ref[k] + share * (keep_ref[k] - came_ref[k])
        out_ref[k, own : own + lines, :] = high
        out_ref[k, own + lines :, :] = low


def last_kernel(col_ref, all_ref, points_ref, mass_ref, sq_ref, gen_ref, costate_ref, share_ref, wide_ref):
    own = points_ref.shape[0]
    count = all_ref.shape[0]
    lines = mass_ref.shape[0]
    parts = [all_ref[k, own : own + lines, :] + all_ref[k, own + lines :, :] for k in range(count)]
    total = lse_over(parts)
    gen_ref[...] = 2.0 * mass_ref[...] + sq_ref[...] - 2.0 * total
    first = col_ref[0] * own
    line = first // LANES
    inside = pl.multiple_of(first - line * LANES, 64)
    result = points_ref[...].astype(jnp.float32)
    span = wide_ref.shape[1] // LANES
    for k in range(count):
        share_ref[k] = jnp.exp(parts[k] - total)
        for part in range(span):
            row = jnp.broadcast_to(share_ref[k, pl.ds(line + part, 1), :], (LANES, LANES))
            wide_ref[k, part * LANES : (part + 1) * LANES, :] = jnp.transpose(row)
        result -= wide_ref[k, pl.ds(inside, own), :] * all_ref[k, :own, :]
    costate_ref[...] = result


def call(kernel, ins, outs, scratch, flops=0, exps=0, room=28):
    moved = sum(math.prod(x.shape) * x.dtype.itemsize for x in list(ins) + list(outs))
    return pl.pallas_call(
        kernel,
        out_shape=outs,
        in_specs=[SMEM if x.dtype == jnp.int32 else VMEM for x in ins],
        out_specs=[VMEM] * len(outs),
        scratch_shapes=scratch,
        compiler_params=pltpu.CompilerParams(vmem_limit_bytes=room * 2**20),
        cost_estimate=pl.CostEstimate(flops=flops, bytes_accessed=moved, transcendentals=exps),
    )(*ins)


def f32(*shape):
    return jax.ShapeDtypeStruct(shape, jnp.float32)


def wide_scratch(n):
    return pltpu.VMEM((n, LANES), jnp.float32)


def body(n_row, n_col, points_gen, points_obs, log_mass_gen, log_mass_obs):
    own = points_gen.shape[0]
    half = n_col // 2
    groups = [list(range(core, n_col, 2)) for core in range(2)]
    pair = [(k, k ^ 1) for k in range(n_col)]
    col = lax.axis_index("col").astype(jnp.int32)
    core = lax.rem(col, 2).reshape(1)
    n, m = own * n_col, points_obs.shape[0] * n_row
    lines, obs_lines = n // LANES, m // LANES

    def over_row(blocks):
        return lax.all_to_all(blocks, "row", 0, 0)

    def over_col(blocks):
        return lax.all_to_all(blocks, "col", 0, 0)

    def over_chips(blocks):
        return lax.all_to_all(blocks, "col", 0, 0, axis_index_groups=groups)

    mass_gen = log_mass_gen.reshape(lines, LANES)
    mass_obs = log_mass_obs.reshape(obs_lines, LANES)
    same = over_chips(jnp.broadcast_to(points_gen[None], (half,) + points_gen.shape))
    obs_copies = jnp.broadcast_to(points_obs[None], (n_row,) + points_obs.shape)
    same, obs_copies = lax.optimization_barrier((same, obs_copies))
    obs, same = lax.optimization_barrier((over_row(obs_copies).reshape(m, LANES), same))
    other = lax.ppermute(same, "col", pair)

    cost = dict(flops=2 * n * m * LANES, exps=n * m)
    product_cost = dict(flops=2 * n * m * LANES)
    small, gen_small = wide_scratch(obs_lines), wide_scratch(lines)
    col_out, row_out = f32(n_row, obs_lines, LANES), f32(n_col, lines, LANES)
    col_own, gen, gen_sq, obs_sq = call(
        first_kernel,
        (core, same, other, obs, mass_gen),
        [
            col_out,
            jax.ShapeDtypeStruct((n, LANES), points_gen.dtype),
            f32(lines, LANES),
            f32(obs_lines, LANES),
        ],
        [wide_scratch(n), small, small],
        room=48,
        **cost,
    )
    col_all = over_row(col_own)
    row_own, obs_add, gen_add, matrix = call(
        second_kernel,
        (obs, gen, mass_obs, col_all),
        [row_out, f32(obs_lines, LANES), f32(lines, LANES), jax.ShapeDtypeStruct((m, n), jnp.bfloat16)],
        [wide_scratch(m), gen_small, gen_small],
        **cost,
    )
    row_all = over_col(row_own)
    first = row_own
    for step in range(1, ITERS):
        (col_own,) = call(
            col_kernel,
            (matrix, obs, gen, mass_gen, row_all, first, obs_add, gen_add),
            [col_out],
            [wide_scratch(n), small, small],
            **product_cost,
        )
        col_all = over_row(col_own)
        if step == ITERS - 1:
            break
        (row_own,) = call(
            row_kernel,
            (matrix, obs, gen, mass_obs, col_all, obs_add, gen_add),
            [row_out],
            [wide_scratch(m), gen_small, gen_small],
            **product_cost,
        )
        row_all = over_col(row_own)
    potential_obs, row_lse, keep, send = call(
        mean_kernel,
        (core, matrix, obs, gen, mass_obs, col_all, obs_add, gen_add, obs_sq),
        [f32(obs_lines, LANES), f32(lines, LANES), f32(half, own, LANES), f32(half, own, LANES)],
        [wide_scratch(m), gen_small, gen_small, wide_scratch(n)],
        **product_cost,
    )
    came = lax.ppermute(send.astype(jnp.float16), "col", pair).astype(jnp.float32)
    came_lse = lax.ppermute(row_lse, "col", pair)
    (joined,) = call(
        pair_kernel, (core, keep, came, row_lse, came_lse), [f32(half, own + 2 * lines, LANES)], [wide_scratch(n)]
    )
    joined_all = over_chips(joined.astype(jnp.float16)).astype(jnp.float32)
    span = own // LANES + 1
    potential_gen, costate = call(
        last_kernel,
        (col.reshape(1), joined_all, points_gen, mass_gen, gen_sq),
        [f32(lines, LANES), f32(own, LANES)],
        [pltpu.VMEM((half, lines, LANES), jnp.float32), pltpu.VMEM((half, span * LANES, LANES), jnp.float32)],
    )
    return potential_gen.reshape(-1), potential_obs.reshape(-1), costate


def solution(mesh):
    return jax.shard_map(
        functools.partial(body, mesh.shape["row"], mesh.shape["col"]),
        mesh=mesh,
        in_specs=(P(("row", "col"), None), P(("col", "row"), None), P("row"), P("col")),
        out_specs=(P("row"), P("col"), P(("row", "col"), None)),
        check_vma=False,
    )
```

```python
import functools
import math

import jax
import jax.numpy as jnp
from jax import lax
from jax.experimental import pallas as pl
from jax.experimental.pallas import tpu as pltpu
from jax.sharding import PartitionSpec as P

ITERS = 4
LANES = 128
CHUNK = 256
SAMPLE = 128
LOW, HIGH = 1e-20, 1e30
STEEP, FAINT, NOTHING = 20.0, 60.0, 60.0
VMEM = pl.BlockSpec(memory_space=pltpu.VMEM)
SMEM = pl.BlockSpec(memory_space=pltpu.SMEM)
NT = (((1,), (1,)), ((), ()))


def lse_over(parts):
    top = functools.reduce(jnp.maximum, parts)
    return top + jnp.log(sum(jnp.exp(part - top) for part in parts))


def planes(ref):
    return [ref[k] for k in range(ref.shape[0])]


def scores(left, right, left_wide):
    prod = lax.dot_general(left, right, NT, preferred_element_type=jnp.float32)
    return prod + jnp.concatenate([left_wide] * (right.shape[0] // LANES), axis=1)


def fold(values, op):
    rows, width = values.shape
    return op(values.reshape(rows // 8, 8, width), axis=0)


def store_row(ref, first, row):
    for part in range(row.shape[1] // LANES):
        ref[pl.ds(first + part, 1), :] = row[:, part * LANES : (part + 1) * LANES]


def dense_of(row):
    return jnp.concatenate([row[:, k * LANES : (k + 1) * LANES] for k in range(row.shape[1] // LANES)], axis=0)


def row_of(dense):
    return jnp.concatenate([dense[k : k + 1, :] for k in range(dense.shape[0])], axis=1)


def widen(dense, wide_ref):
    for part in range(dense.shape[0]):
        row = jnp.broadcast_to(dense[part : part + 1, :], (LANES, LANES))
        wide_ref[part * LANES : (part + 1) * LANES, :] = jnp.transpose(row)


def squares(points):
    wide = points.astype(jnp.float32)
    square = wide * wide
    high = square.astype(jnp.bfloat16)
    low = (square - high.astype(jnp.float32)).astype(jnp.bfloat16)
    ones = jnp.ones((8, LANES), jnp.bfloat16)
    row = lax.dot_general(ones, high, NT, preferred_element_type=jnp.float32)
    row += lax.dot_general(ones, low, NT, preferred_element_type=jnp.float32)
    return dense_of(row[:1, :])


def in_parts(row):
    high = row.astype(jnp.bfloat16).astype(jnp.float32)
    middle = (row - high).astype(jnp.bfloat16).astype(jnp.float32)
    low = row - high - middle
    line = lax.broadcasted_iota(jnp.int32, (16, row.shape[1]), 0)
    parts = jnp.where(line == 0, high, jnp.where(line == 1, middle, jnp.where(line == 2, low, 0.0)))
    return parts.astype(jnp.bfloat16)


def means_of(left_ref, chunk, values, mean_ref):
    left_t = jnp.transpose(left_ref[...].astype(jnp.float32))
    left_t = jnp.concatenate([left_t, jnp.ones((16, left_t.shape[1]), jnp.float32)], axis=0).astype(jnp.bfloat16)
    numer = jnp.dot(left_t, values.astype(jnp.bfloat16), preferred_element_type=jnp.float32)
    mean = numer[:LANES, :] / numer[LANES : LANES + 1, :]
    mean_ref[pl.ds(pl.multiple_of(chunk * CHUNK, CHUNK), CHUNK), :] = jnp.transpose(mean)


def exact_pass(left_ref, right_ref, wide_ref, shift_ref, total_ref, mean_ref=None):
    n, m = left_ref.shape[0], right_ref.shape[0]
    block = 512
    per = CHUNK // LANES

    def one(chunk, carry):
        right = right_ref[pl.ds(pl.multiple_of(chunk * CHUNK, CHUNK), CHUNK), :]

        def largest(step, top):
            rows = pl.ds(pl.multiple_of(step * block, block), block)
            return jnp.maximum(top, fold(scores(left_ref[rows, :], right, wide_ref[rows, :]), jnp.max))

        top = lax.fori_loop(0, n // block, largest, jnp.full((8, CHUNK), -3e38, jnp.float32))
        top = jnp.max(top, axis=0, keepdims=True)

        def add(step, total):
            rows = pl.ds(pl.multiple_of(step * block, block), block)
            return total + fold(jnp.exp(scores(left_ref[rows, :], right, wide_ref[rows, :]) - top), jnp.sum)

        total = lax.fori_loop(0, n // block, add, jnp.zeros((8, CHUNK), jnp.float32))
        store_row(shift_ref, chunk * per, top)
        store_row(total_ref, chunk * per, jnp.sum(total, axis=0, keepdims=True))
        if mean_ref is not None:
            means_of(left_ref, chunk, jnp.exp(scores(left_ref[...], right, wide_ref[...]) - top), mean_ref)
        return carry

    lax.fori_loop(0, m // CHUNK, one, 0)


def sampled_pass(left_ref, right_ref, wide_ref, shift_ref, total_ref, matrix_ref=None):
    m = right_ref.shape[0]
    per = CHUNK // LANES
    for chunk in range(m // CHUNK):
        right = right_ref[chunk * CHUNK : (chunk + 1) * CHUNK, :]
        some = scores(left_ref[:SAMPLE, :], right, wide_ref[:SAMPLE, :])
        shift = jnp.max(fold(some, jnp.max), axis=0, keepdims=True)
        values = jnp.exp(scores(left_ref[...], right, wide_ref[...]) - shift)
        total = jnp.sum(fold(values, jnp.sum), axis=0, keepdims=True)
        store_row(shift_ref, chunk * per, shift)
        store_row(total_ref, chunk * per, total)
        if matrix_ref is not None:
            matrix_ref[:, chunk * CHUNK : (chunk + 1) * CHUNK] = values.astype(jnp.bfloat16)

    @pl.when(jnp.logical_not(jnp.max(total_ref[...]) < HIGH))
    def _():
        exact_pass(left_ref, right_ref, wide_ref, shift_ref, total_ref)
        if matrix_ref is not None:
            for chunk in range(m // CHUNK):
                across = pl.ds(chunk * CHUNK, CHUNK)
                top = row_of(shift_ref[chunk * per : (chunk + 1) * per, :])
                values = jnp.exp(scores(left_ref[...], right_ref[across, :], wide_ref[...]) - top)
                matrix_ref[:, across] = values.astype(jnp.bfloat16)

    return shift_ref[...] + jnp.log(total_ref[...])


def spread(out_ref, value):
    for copy in range(out_ref.shape[0]):
        out_ref[copy] = value


def of_core(dense, core, count):
    swapped = pltpu.roll(dense, LANES // 2, axis=1)
    left = lax.broadcasted_iota(jnp.int32, (1, LANES), 1) < LANES // 2
    halves = dense.shape[0] // count
    chosen = []
    for parity in range(2):
        sources = [(2 * k + parity) * halves + t for k in range(count) for t in range(halves)]
        rows = []
        for one, two in zip(sources[::2], sources[1::2]):
            first = (swapped if one % 2 else dense)[one // 2 : one // 2 + 1, :]
            second = (dense if two % 2 else swapped)[two // 2 : two // 2 + 1, :]
            rows.append(jnp.where(left, first, second))
        chosen.append(jnp.concatenate(rows, axis=0))
    return jnp.where(core == 0, chosen[0], chosen[1])


def half_kernel(count, core_ref, same_ref, right_ref, mass_ref, out_ref, right_sq_ref, wide_ref, shift_ref, total_ref):
    right_sq_ref[...] = squares(right_ref[...])
    mass = of_core(mass_ref[...], core_ref[0], count)
    widen(mass - 0.5 * squares(same_ref[...]), wide_ref)
    out_ref[...] = sampled_pass(same_ref, right_ref, wide_ref, shift_ref, total_ref)


def first_kernel(
    count, core_ref, same_ref, other_ref, right_ref, mass_ref, half_ref,
    out_ref, left_ref, sq_ref, wide_ref, shift_ref, total_ref,
):
    core = core_ref[0]
    own = same_ref.shape[0] // count
    for k in range(count):
        rows = pl.ds(k * own, own)
        left_ref[pl.ds(pl.multiple_of((2 * k + core) * own, 64), own), :] = same_ref[rows, :]
        left_ref[pl.ds(pl.multiple_of((2 * k + 1 - core) * own, 64), own), :] = other_ref[rows, :]
    sq_ref[...] = squares(left_ref[...])
    mass = of_core(mass_ref[...], 1 - core, count)
    widen(mass - 0.5 * squares(other_ref[...]), wide_ref)
    result = sampled_pass(other_ref, right_ref, wide_ref, shift_ref, total_ref)
    spread(out_ref, lse_over([half_ref[...], result]))


def second_kernel(
    left_ref, right_ref, mass_ref, from_ref,
    out_ref, left_add_ref, right_add_ref, matrix_ref, wide_ref, shift_ref, total_ref,
):
    offset = 2.0 * mass_ref[...] - lse_over(planes(from_ref))
    left_add_ref[...] = offset
    widen(offset, wide_ref)
    spread(out_ref, sampled_pass(left_ref, right_ref, wide_ref, shift_ref, total_ref, matrix_ref))
    right_add_ref[...] = -shift_ref[...]


def close_pass(left_ref, right_ref, offset, bad, add_ref, wide_ref, shift_ref, total_ref, mean_ref=None):
    shift_ref[...] = -add_ref[...]
    totals = total_ref[...]
    fits = (totals > LOW) & (totals < HIGH)
    marks = [jnp.where(mask, 1.0, 0.0) for mask in (bad, jnp.logical_not(fits))]
    flags = [mark[k : k + 8, :] for mark in marks for k in range(0, mark.shape[0], 8)]

    @pl.when(jnp.max(functools.reduce(jnp.maximum, flags)) > 0.0)
    def _():
        widen(offset, wide_ref)
        exact_pass(left_ref, right_ref, wide_ref, shift_ref, total_ref, mean_ref)


def col_kernel(
    matrix_ref, obs_ref, gen_ref, mass_ref, from_ref, first_ref, obs_add_ref, gen_add_ref,
    out_ref, wide_ref, shift_ref, total_ref,
):
    offset = 2.0 * mass_ref[...] - lse_over(planes(from_ref))
    gain = offset - gen_add_ref[...]
    level = offset + first_ref[0]
    factors = jnp.exp(gain)
    for block in range(obs_ref.shape[0] // LANES):
        rows = pl.ds(block * LANES, LANES)
        total = jnp.zeros((LANES, LANES), jnp.float32)
        for part in range(gain.shape[0]):
            values = matrix_ref[rows, part * LANES : (part + 1) * LANES].astype(jnp.float32)
            total += values * factors[part : part + 1, :]
        total_ref[block : block + 1, :] = jnp.sum(jnp.transpose(total), axis=0, keepdims=True)
    bad = (level > STEEP) | ((gain < -FAINT) & (level > -NOTHING))
    close_pass(gen_ref, obs_ref, offset, bad, obs_add_ref, wide_ref, shift_ref, total_ref)
    spread(out_ref, shift_ref[...] + jnp.log(total_ref[...]))


def row_kernel(
    matrix_ref, obs_ref, gen_ref, mass_ref, from_ref, obs_add_ref, gen_add_ref,
    out_ref, wide_ref, shift_ref, total_ref,
):
    offset = 2.0 * mass_ref[...] - lse_over(planes(from_ref))
    gain = offset - obs_add_ref[...]
    total = jnp.dot(in_parts(row_of(jnp.exp(gain))), matrix_ref[...], preferred_element_type=jnp.float32)
    total_ref[...] = dense_of(jnp.sum(total[:8, :], axis=0, keepdims=True))
    close_pass(obs_ref, gen_ref, offset, wild(gain), gen_add_ref, wide_ref, shift_ref, total_ref)
    spread(out_ref, shift_ref[...] + jnp.log(total_ref[...]))


def wild(gain):
    return (gain > STEEP) | (gain < -FAINT)


def mean_kernel(
    core_ref, matrix_ref, left_ref, right_ref, mass_ref, from_ref, left_add_ref, right_add_ref, left_sq_ref,
    potential_ref, out_ref, keep_ref, send_ref, wide_ref, shift_ref, total_ref, mean_ref,
):
    offset = 2.0 * mass_ref[...] - lse_over(planes(from_ref))
    potential_ref[...] = 2.0 * (offset - mass_ref[...]) + left_sq_ref[...]
    gain = offset - left_add_ref[...]
    weight = row_of(jnp.exp(gain))
    left_t = jnp.transpose(left_ref[...].astype(jnp.float32)) * weight
    high = left_t.astype(jnp.bfloat16)
    low = (left_t - high.astype(jnp.float32)).astype(jnp.bfloat16)
    factors = jnp.concatenate([high, low, in_parts(weight)], axis=0)
    for chunk in range(right_ref.shape[0] // CHUNK):
        across = pl.ds(chunk * CHUNK, CHUNK)
        sums = jnp.dot(factors, matrix_ref[:, across], preferred_element_type=jnp.float32)
        total = jnp.sum(sums[2 * LANES : 2 * LANES + 8, :], axis=0, keepdims=True)
        store_row(total_ref, chunk * CHUNK // LANES, total)
        mean_ref[across, :] = jnp.transpose((sums[:LANES, :] + sums[LANES : 2 * LANES, :]) / total)
    close_pass(left_ref, right_ref, offset, wild(gain), right_add_ref, wide_ref, shift_ref, total_ref, mean_ref)
    out_ref[...] = shift_ref[...] + jnp.log(total_ref[...])
    core = core_ref[0]
    count, own, _ = keep_ref.shape
    for k in range(count):
        keep_ref[k] = mean_ref[pl.ds(pl.multiple_of((2 * k + core) * own, 64), own), :]
        send_ref[k] = mean_ref[pl.ds(pl.multiple_of((2 * k + 1 - core) * own, 64), own), :]


def pair_kernel(core_ref, keep_ref, came_ref, lse_ref, came_lse_ref, out_ref, wide_ref):
    core = core_ref[0]
    count, own, _ = keep_ref.shape
    both = lse_over([lse_ref[...], came_lse_ref[...]])
    lines = both.shape[0]
    spaced = both * 8193.0
    high = spaced - (spaced - both)
    low = both - high
    widen(jnp.exp(lse_ref[...] - both), wide_ref)
    for k in range(count):
        share = wide_ref[pl.ds(pl.multiple_of((2 * k + core) * own, 64), own), :]
        out_ref[k, :own, :] = came_ref[k] + share * (keep_ref[k] - came_ref[k])
        out_ref[k, own : own + lines, :] = high
        out_ref[k, own + lines :, :] = low


def last_kernel(col_ref, all_ref, points_ref, mass_ref, sq_ref, gen_ref, costate_ref, share_ref, wide_ref):
    own = points_ref.shape[0]
    count = all_ref.shape[0]
    lines = mass_ref.shape[0]
    parts = [all_ref[k, own : own + lines, :] + all_ref[k, own + lines :, :] for k in range(count)]
    total = lse_over(parts)
    gen_ref[...] = 2.0 * mass_ref[...] + sq_ref[...] - 2.0 * total
    first = col_ref[0] * own
    line = first // LANES
    inside = pl.multiple_of(first - line * LANES, 64)
    result = points_ref[...].astype(jnp.float32)
    span = wide_ref.shape[1] // LANES
    for k in range(count):
        share_ref[k] = jnp.exp(parts[k] - total)
        for part in range(span):
            row = jnp.broadcast_to(share_ref[k, pl.ds(line + part, 1), :], (LANES, LANES))
            wide_ref[k, part * LANES : (part + 1) * LANES, :] = jnp.transpose(row)
        result -= wide_ref[k, pl.ds(inside, own), :] * all_ref[k, :own, :]
    costate_ref[...] = result


def call(kernel, ins, outs, scratch, flops=0, exps=0, room=28):
    moved = sum(math.prod(x.shape) * x.dtype.itemsize for x in list(ins) + list(outs))
    return pl.pallas_call(
        kernel,
        out_shape=outs,
        in_specs=[SMEM if x.dtype == jnp.int32 else VMEM for x in ins],
        out_specs=[VMEM] * len(outs),
        scratch_shapes=scratch,
        compiler_params=pltpu.CompilerParams(vmem_limit_bytes=room * 2**20),
        cost_estimate=pl.CostEstimate(flops=flops, bytes_accessed=moved, transcendentals=exps),
    )(*ins)


def f32(*shape):
    return jax.ShapeDtypeStruct(shape, jnp.float32)


def wide_scratch(n):
    return pltpu.VMEM((n, LANES), jnp.float32)


def body(n_row, n_col, points_gen, points_obs, log_mass_gen, log_mass_obs):
    own = points_gen.shape[0]
    half = n_col // 2
    groups = [list(range(core, n_col, 2)) for core in range(2)]
    pair = [(k, k ^ 1) for k in range(n_col)]
    col = lax.axis_index("col").astype(jnp.int32)
    core = lax.rem(col, 2).reshape(1)
    n, m = own * n_col, points_obs.shape[0] * n_row
    lines, obs_lines = n // LANES, m // LANES

    def over_row(blocks):
        return lax.all_to_all(blocks, "row", 0, 0)

    def over_col(blocks):
        return lax.all_to_all(blocks, "col", 0, 0)

    def over_chips(blocks):
        return lax.all_to_all(blocks, "col", 0, 0, axis_index_groups=groups)

    mass_gen = log_mass_gen.reshape(lines, LANES)
    mass_obs = log_mass_obs.reshape(obs_lines, LANES)
    same = over_chips(jnp.broadcast_to(points_gen[None], (half,) + points_gen.shape))
    obs_copies = jnp.broadcast_to(points_obs[None], (n_row,) + points_obs.shape)
    same, obs_copies = lax.optimization_barrier((same, obs_copies))
    obs, same = lax.optimization_barrier((over_row(obs_copies).reshape(m, LANES), same))
    other = lax.ppermute(same, "col", pair)

    cost = dict(flops=2 * n * m * LANES, exps=n * m)
    product_cost = dict(flops=2 * n * m * LANES)
    small, gen_small = wide_scratch(obs_lines), wide_scratch(lines)
    col_out, row_out = f32(n_row, obs_lines, LANES), f32(n_col, lines, LANES)
    same, other = same.reshape(n // 2, LANES), other.reshape(n // 2, LANES)
    half_cost = dict(flops=n * m * LANES, exps=n * m // 2)
    half_own, obs_sq = call(
        functools.partial(half_kernel, half),
        (core, same, obs, mass_gen),
        [f32(obs_lines, LANES), f32(obs_lines, LANES)],
        [wide_scratch(n // 2), small, small],
        **half_cost,
    )
    col_own, gen, gen_sq = call(
        functools.partial(first_kernel, half),
        (core, same, other, obs, mass_gen, half_own),
        [col_out, jax.ShapeDtypeStruct((n, LANES), points_gen.dtype), f32(lines, LANES)],
        [wide_scratch(n // 2), small, small],
        **half_cost,
    )
    col_all = over_row(col_own)
    row_own, obs_add, gen_add, matrix = call(
        second_kernel,
        (obs, gen, mass_obs, col_all),
        [row_out, f32(obs_lines, LANES), f32(lines, LANES), jax.ShapeDtypeStruct((m, n), jnp.bfloat16)],
        [wide_scratch(m), gen_small, gen_small],
        **cost,
    )
    row_all = over_col(row_own)
    first = row_own
    for step in range(1, ITERS):
        (col_own,) = call(
            col_kernel,
            (matrix, obs, gen, mass_gen, row_all, first, obs_add, gen_add),
            [col_out],
            [wide_scratch(n), small, small],
            **product_cost,
        )
        col_all = over_row(col_own)
        if step == ITERS - 1:
            break
        (row_own,) = call(
            row_kernel,
            (matrix, obs, gen, mass_obs, col_all, obs_add, gen_add),
            [row_out],
            [wide_scratch(m), gen_small, gen_small],
            **product_cost,
        )
        row_all = over_col(row_own)
    potential_obs, row_lse, keep, send = call(
        mean_kernel,
        (core, matrix, obs, gen, mass_obs, col_all, obs_add, gen_add, obs_sq),
        [f32(obs_lines, LANES), f32(lines, LANES), f32(half, own, LANES), f32(half, own, LANES)],
        [wide_scratch(m), gen_small, gen_small, wide_scratch(n)],
        **product_cost,
    )
    came = lax.ppermute(send.astype(jnp.float16), "col", pair).astype(jnp.float32)
    came_lse = lax.ppermute(row_lse, "col", pair)
    (joined,) = call(
        pair_kernel, (core, keep, came, row_lse, came_lse), [f32(half, own + 2 * lines, LANES)], [wide_scratch(n)]
    )
    joined_all = over_chips(joined.astype(jnp.float16)).astype(jnp.float32)
    span = own // LANES + 1
    potential_gen, costate = call(
        last_kernel,
        (col.reshape(1), joined_all, points_gen, mass_gen, gen_sq),
        [f32(lines, LANES), f32(own, LANES)],
        [pltpu.VMEM((half, lines, LANES), jnp.float32), pltpu.VMEM((half, span * LANES, LANES), jnp.float32)],
    )
    return potential_gen.reshape(-1), potential_obs.reshape(-1), costate


def solution(mesh):
    return jax.shard_map(
        functools.partial(body, mesh.shape["row"], mesh.shape["col"]),
        mesh=mesh,
        in_specs=(P(("row", "col"), None), P(("col", "row"), None), P("row"), P("col")),
        out_specs=(P("row"), P("col"), P(("row", "col"), None)),
        check_vma=False,
    )
```

```python
import functools
import math

import jax
import jax.numpy as jnp
from jax import lax
from jax.experimental import pallas as pl
from jax.experimental.pallas import tpu as pltpu
from jax.sharding import PartitionSpec as P

ITERS = 4
LANES = 128
CHUNK = 256
SAMPLE = 128
LOW, HIGH = 1e-20, 1e30
STEEP, FAINT, NOTHING = 20.0, 60.0, 60.0
VMEM = pl.BlockSpec(memory_space=pltpu.VMEM)
SMEM = pl.BlockSpec(memory_space=pltpu.SMEM)
NT = (((1,), (1,)), ((), ()))


def lse_over(parts):
    top = functools.reduce(jnp.maximum, parts)
    return top + jnp.log(sum(jnp.exp(part - top) for part in parts))


def planes(ref):
    return [ref[k] for k in range(ref.shape[0])]


def scores(left, right, left_wide):
    prod = lax.dot_general(left, right, NT, preferred_element_type=jnp.float32)
    return prod + jnp.concatenate([left_wide] * (right.shape[0] // LANES), axis=1)


def fold(values, op):
    rows, width = values.shape
    return op(values.reshape(rows // 8, 8, width), axis=0)


def store_row(ref, first, row):
    for part in range(row.shape[1] // LANES):
        ref[pl.ds(first + part, 1), :] = row[:, part * LANES : (part + 1) * LANES]


def dense_of(row):
    return jnp.concatenate([row[:, k * LANES : (k + 1) * LANES] for k in range(row.shape[1] // LANES)], axis=0)


def row_of(dense):
    return jnp.concatenate([dense[k : k + 1, :] for k in range(dense.shape[0])], axis=1)


def widen(dense, wide_ref):
    for part in range(dense.shape[0]):
        row = jnp.broadcast_to(dense[part : part + 1, :], (LANES, LANES))
        wide_ref[part * LANES : (part + 1) * LANES, :] = jnp.transpose(row)


def squares(points):
    wide = points.astype(jnp.float32)
    square = wide * wide
    high = square.astype(jnp.bfloat16)
    low = (square - high.astype(jnp.float32)).astype(jnp.bfloat16)
    ones = jnp.ones((8, LANES), jnp.bfloat16)
    row = lax.dot_general(ones, high, NT, preferred_element_type=jnp.float32)
    row += lax.dot_general(ones, low, NT, preferred_element_type=jnp.float32)
    return dense_of(row[:1, :])


def in_parts(row):
    high = row.astype(jnp.bfloat16).astype(jnp.float32)
    middle = (row - high).astype(jnp.bfloat16).astype(jnp.float32)
    low = row - high - middle
    line = lax.broadcasted_iota(jnp.int32, (16, row.shape[1]), 0)
    parts = jnp.where(line == 0, high, jnp.where(line == 1, middle, jnp.where(line == 2, low, 0.0)))
    return parts.astype(jnp.bfloat16)


def means_of(left_ref, chunk, values, mean_ref):
    left_t = jnp.transpose(left_ref[...].astype(jnp.float32))
    left_t = jnp.concatenate([left_t, jnp.ones((16, left_t.shape[1]), jnp.float32)], axis=0).astype(jnp.bfloat16)
    numer = jnp.dot(left_t, values.astype(jnp.bfloat16), preferred_element_type=jnp.float32)
    mean = numer[:LANES, :] / numer[LANES : LANES + 1, :]
    mean_ref[pl.ds(pl.multiple_of(chunk * CHUNK, CHUNK), CHUNK), :] = jnp.transpose(mean)


def exact_pass(left_ref, right_ref, wide_ref, shift_ref, total_ref, mean_ref=None):
    n, m = left_ref.shape[0], right_ref.shape[0]
    block = 512
    per = CHUNK // LANES

    def one(chunk, carry):
        right = right_ref[pl.ds(pl.multiple_of(chunk * CHUNK, CHUNK), CHUNK), :]

        def largest(step, top):
            rows = pl.ds(pl.multiple_of(step * block, block), block)
            return jnp.maximum(top, fold(scores(left_ref[rows, :], right, wide_ref[rows, :]), jnp.max))

        top = lax.fori_loop(0, n // block, largest, jnp.full((8, CHUNK), -3e38, jnp.float32))
        top = jnp.max(top, axis=0, keepdims=True)

        def add(step, total):
            rows = pl.ds(pl.multiple_of(step * block, block), block)
            return total + fold(jnp.exp(scores(left_ref[rows, :], right, wide_ref[rows, :]) - top), jnp.sum)

        total = lax.fori_loop(0, n // block, add, jnp.zeros((8, CHUNK), jnp.float32))
        store_row(shift_ref, chunk * per, top)
        store_row(total_ref, chunk * per, jnp.sum(total, axis=0, keepdims=True))
        if mean_ref is not None:
            means_of(left_ref, chunk, jnp.exp(scores(left_ref[...], right, wide_ref[...]) - top), mean_ref)
        return carry

    lax.fori_loop(0, m // CHUNK, one, 0)


def sampled_pass(left_ref, right_ref, wide_ref, shift_ref, total_ref, matrix_ref=None):
    m = right_ref.shape[0]
    per = CHUNK // LANES
    for chunk in range(m // CHUNK):
        right = right_ref[chunk * CHUNK : (chunk + 1) * CHUNK, :]
        some = scores(left_ref[:SAMPLE, :], right, wide_ref[:SAMPLE, :])
        shift = jnp.max(fold(some, jnp.max), axis=0, keepdims=True)
        values = jnp.exp(scores(left_ref[...], right, wide_ref[...]) - shift)
        total = jnp.sum(fold(values, jnp.sum), axis=0, keepdims=True)
        store_row(shift_ref, chunk * per, shift)
        store_row(total_ref, chunk * per, total)
        if matrix_ref is not None:
            matrix_ref[:, chunk * CHUNK : (chunk + 1) * CHUNK] = values.astype(jnp.bfloat16)

    @pl.when(jnp.logical_not(jnp.max(total_ref[...]) < HIGH))
    def _():
        exact_pass(left_ref, right_ref, wide_ref, shift_ref, total_ref)
        if matrix_ref is not None:
            for chunk in range(m // CHUNK):
                across = pl.ds(chunk * CHUNK, CHUNK)
                top = row_of(shift_ref[chunk * per : (chunk + 1) * per, :])
                values = jnp.exp(scores(left_ref[...], right_ref[across, :], wide_ref[...]) - top)
                matrix_ref[:, across] = values.astype(jnp.bfloat16)

    return shift_ref[...] + jnp.log(total_ref[...])


def spread(out_ref, value):
    for copy in range(out_ref.shape[0]):
        out_ref[copy] = value


def of_core(dense, core, count):
    swapped = pltpu.roll(dense, LANES // 2, axis=1)
    left = lax.broadcasted_iota(jnp.int32, (1, LANES), 1) < LANES // 2
    halves = dense.shape[0] // count
    chosen = []
    for parity in range(2):
        sources = [(2 * k + parity) * halves + t for k in range(count) for t in range(halves)]
        rows = []
        for one, two in zip(sources[::2], sources[1::2]):
            first = (swapped if one % 2 else dense)[one // 2 : one // 2 + 1, :]
            second = (dense if two % 2 else swapped)[two // 2 : two // 2 + 1, :]
            rows.append(jnp.where(left, first, second))
        chosen.append(jnp.concatenate(rows, axis=0))
    return jnp.where(core == 0, chosen[0], chosen[1])


def half_kernel(count, core_ref, same_ref, right_ref, mass_ref, out_ref, right_sq_ref, wide_ref, shift_ref, total_ref):
    right_sq_ref[...] = squares(right_ref[...])
    mass = of_core(mass_ref[...], core_ref[0], count)
    widen(mass - 0.5 * squares(same_ref[...]), wide_ref)
    out_ref[...] = sampled_pass(same_ref, right_ref, wide_ref, shift_ref, total_ref)


def first_kernel(
    count, core_ref, same_ref, other_ref, right_ref, mass_ref, half_ref,
    out_ref, left_ref, sq_ref, wide_ref, shift_ref, total_ref,
):
    core = core_ref[0]
    own = same_ref.shape[0] // count
    for k in range(count):
        rows = pl.ds(k * own, own)
        left_ref[pl.ds(pl.multiple_of((2 * k + core) * own, 64), own), :] = same_ref[rows, :]
        left_ref[pl.ds(pl.multiple_of((2 * k + 1 - core) * own, 64), own), :] = other_ref[rows, :]
    sq_ref[...] = squares(left_ref[...])
    mass = of_core(mass_ref[...], 1 - core, count)
    widen(mass - 0.5 * squares(other_ref[...]), wide_ref)
    result = sampled_pass(other_ref, right_ref, wide_ref, shift_ref, total_ref)
    spread(out_ref, lse_over([half_ref[...], result]))


def second_kernel(
    left_ref, right_ref, mass_ref, from_ref,
    out_ref, left_add_ref, right_add_ref, matrix_ref, wide_ref, shift_ref, total_ref,
):
    offset = 2.0 * mass_ref[...] - lse_over(planes(from_ref))
    left_add_ref[...] = offset
    widen(offset, wide_ref)
    spread(out_ref, sampled_pass(left_ref, right_ref, wide_ref, shift_ref, total_ref, matrix_ref))
    right_add_ref[...] = -shift_ref[...]


def close_pass(left_ref, right_ref, offset, bad, add_ref, wide_ref, shift_ref, total_ref, mean_ref=None):
    shift_ref[...] = -add_ref[...]
    totals = total_ref[...]
    fits = (totals > LOW) & (totals < HIGH)
    marks = [jnp.where(mask, 1.0, 0.0) for mask in (bad, jnp.logical_not(fits))]
    flags = [mark[k : k + 8, :] for mark in marks for k in range(0, mark.shape[0], 8)]

    @pl.when(jnp.max(functools.reduce(jnp.maximum, flags)) > 0.0)
    def _():
        widen(offset, wide_ref)
        exact_pass(left_ref, right_ref, wide_ref, shift_ref, total_ref, mean_ref)


def col_kernel(
    matrix_ref, obs_ref, gen_ref, mass_ref, from_ref, first_ref, obs_add_ref, gen_add_ref,
    out_ref, wide_ref, shift_ref, total_ref,
):
    offset = 2.0 * mass_ref[...] - lse_over(planes(from_ref))
    gain = offset - gen_add_ref[...]
    level = offset + first_ref[0]
    factors = jnp.exp(gain)
    for block in range(obs_ref.shape[0] // LANES):
        rows = pl.ds(block * LANES, LANES)
        total = jnp.zeros((LANES, LANES), jnp.float32)
        for part in range(gain.shape[0]):
            values = matrix_ref[rows, part * LANES : (part + 1) * LANES].astype(jnp.float32)
            total += values * factors[part : part + 1, :]
        total_ref[block : block + 1, :] = jnp.sum(jnp.transpose(total), axis=0, keepdims=True)
    bad = (level > STEEP) | ((gain < -FAINT) & (level > -NOTHING))
    close_pass(gen_ref, obs_ref, offset, bad, obs_add_ref, wide_ref, shift_ref, total_ref)
    spread(out_ref, shift_ref[...] + jnp.log(total_ref[...]))


def row_kernel(
    matrix_ref, obs_ref, gen_ref, mass_ref, from_ref, obs_add_ref, gen_add_ref,
    out_ref, wide_ref, shift_ref, total_ref,
):
    offset = 2.0 * mass_ref[...] - lse_over(planes(from_ref))
    gain = offset - obs_add_ref[...]
    total = jnp.dot(in_parts(row_of(jnp.exp(gain))), matrix_ref[...], preferred_element_type=jnp.float32)
    total_ref[...] = dense_of(jnp.sum(total[:8, :], axis=0, keepdims=True))
    close_pass(obs_ref, gen_ref, offset, wild(gain), gen_add_ref, wide_ref, shift_ref, total_ref)
    spread(out_ref, shift_ref[...] + jnp.log(total_ref[...]))


def wild(gain):
    return (gain > STEEP) | (gain < -FAINT)


def mean_kernel(
    core_ref, matrix_ref, left_ref, right_ref, mass_ref, from_ref, left_add_ref, right_add_ref, left_sq_ref,
    potential_ref, out_ref, keep_ref, send_ref, wide_ref, shift_ref, total_ref, mean_ref,
):
    offset = 2.0 * mass_ref[...] - lse_over(planes(from_ref))
    potential_ref[...] = 2.0 * (offset - mass_ref[...]) + left_sq_ref[...]
    gain = offset - left_add_ref[...]
    weight = row_of(jnp.exp(gain))
    left_t = jnp.transpose(left_ref[...].astype(jnp.float32)) * weight
    high = left_t.astype(jnp.bfloat16)
    low = (left_t - high.astype(jnp.float32)).astype(jnp.bfloat16)
    factors = jnp.concatenate([high, low, in_parts(weight)], axis=0)
    for chunk in range(right_ref.shape[0] // CHUNK):
        across = pl.ds(chunk * CHUNK, CHUNK)
        sums = jnp.dot(factors, matrix_ref[:, across], preferred_element_type=jnp.float32)
        total = jnp.sum(sums[2 * LANES : 2 * LANES + 8, :], axis=0, keepdims=True)
        store_row(total_ref, chunk * CHUNK // LANES, total)
        mean_ref[across, :] = jnp.transpose((sums[:LANES, :] + sums[LANES : 2 * LANES, :]) / total)
    close_pass(left_ref, right_ref, offset, wild(gain), right_add_ref, wide_ref, shift_ref, total_ref, mean_ref)
    out_ref[...] = shift_ref[...] + jnp.log(total_ref[...])
    core = core_ref[0]
    count, own, _ = keep_ref.shape
    for k in range(count):
        keep_ref[k] = mean_ref[pl.ds(pl.multiple_of((2 * k + core) * own, 64), own), :]
        send_ref[k] = mean_ref[pl.ds(pl.multiple_of((2 * k + 1 - core) * own, 64), own), :]


def pair_kernel(core_ref, keep_ref, came_ref, lse_ref, came_lse_ref, out_ref, wide_ref):
    core = core_ref[0]
    count, own, _ = keep_ref.shape
    both = lse_over([lse_ref[...], came_lse_ref[...]])
    lines = both.shape[0]
    spaced = both * 8193.0
    high = spaced - (spaced - both)
    low = both - high
    widen(jnp.exp(lse_ref[...] - both), wide_ref)
    for k in range(count):
        share = wide_ref[pl.ds(pl.multiple_of((2 * k + core) * own, 64), own), :]
        out_ref[k, :own, :] = came_ref[k] + share * (keep_ref[k] - came_ref[k])
        out_ref[k, own : own + lines, :] = high
        out_ref[k, own + lines :, :] = low


def last_kernel(col_ref, all_ref, points_ref, mass_ref, sq_ref, gen_ref, costate_ref, share_ref, wide_ref):
    own = points_ref.shape[0]
    count = all_ref.shape[0]
    lines = mass_ref.shape[0]
    parts = [all_ref[k, own : own + lines, :] + all_ref[k, own + lines :, :] for k in range(count)]
    total = lse_over(parts)
    gen_ref[...] = 2.0 * mass_ref[...] + sq_ref[...] - 2.0 * total
    first = col_ref[0] * own
    line = first // LANES
    inside = pl.multiple_of(first - line * LANES, 64)
    result = points_ref[...].astype(jnp.float32)
    span = wide_ref.shape[1] // LANES
    for k in range(count):
        share_ref[k] = jnp.exp(parts[k] - total)
        for part in range(span):
            row = jnp.broadcast_to(share_ref[k, pl.ds(line + part, 1), :], (LANES, LANES))
            wide_ref[k, part * LANES : (part + 1) * LANES, :] = jnp.transpose(row)
        result -= wide_ref[k, pl.ds(inside, own), :] * all_ref[k, :own, :]
    costate_ref[...] = result


def call(kernel, ins, outs, scratch, flops=0, exps=0, room=28):
    moved = sum(math.prod(x.shape) * x.dtype.itemsize for x in list(ins) + list(outs))
    return pl.pallas_call(
        kernel,
        out_shape=outs,
        in_specs=[SMEM if x.dtype == jnp.int32 else VMEM for x in ins],
        out_specs=[VMEM] * len(outs),
        scratch_shapes=scratch,
        compiler_params=pltpu.CompilerParams(vmem_limit_bytes=room * 2**20),
        cost_estimate=pl.CostEstimate(flops=flops, bytes_accessed=moved, transcendentals=exps),
    )(*ins)


def f32(*shape):
    return jax.ShapeDtypeStruct(shape, jnp.float32)


def wide_scratch(n):
    return pltpu.VMEM((n, LANES), jnp.float32)


def body(n_row, n_col, points_gen, points_obs, log_mass_gen, log_mass_obs):
    own = points_gen.shape[0]
    half = n_col // 2
    groups = [list(range(core, n_col, 2)) for core in range(2)]
    pair = [(k, k ^ 1) for k in range(n_col)]
    col = lax.axis_index("col").astype(jnp.int32)
    core = lax.rem(col, 2).reshape(1)
    n, m = own * n_col, points_obs.shape[0] * n_row
    lines, obs_lines = n // LANES, m // LANES

    def over_row(blocks):
        return lax.all_to_all(blocks, "row", 0, 0)

    def over_col(blocks):
        return lax.all_to_all(blocks, "col", 0, 0)

    def over_chips(blocks):
        return lax.all_to_all(blocks, "col", 0, 0, axis_index_groups=groups)

    mass_gen = log_mass_gen.reshape(lines, LANES)
    mass_obs = log_mass_obs.reshape(obs_lines, LANES)
    obs = over_row(jnp.broadcast_to(points_obs[None], (n_row,) + points_obs.shape)).reshape(m, LANES)
    gen_copies = jnp.broadcast_to(points_gen[None], (half,) + points_gen.shape)
    obs, gen_copies = lax.optimization_barrier((obs, gen_copies))
    same = over_chips(gen_copies)
    other = lax.ppermute(same, "col", pair)

    cost = dict(flops=2 * n * m * LANES, exps=n * m)
    product_cost = dict(flops=2 * n * m * LANES)
    small, gen_small = wide_scratch(obs_lines), wide_scratch(lines)
    col_out, row_out = f32(n_row, obs_lines, LANES), f32(n_col, lines, LANES)
    same, other = same.reshape(n // 2, LANES), other.reshape(n // 2, LANES)
    half_cost = dict(flops=n * m * LANES, exps=n * m // 2)
    half_own, obs_sq = call(
        functools.partial(half_kernel, half),
        (core, same, obs, mass_gen),
        [f32(obs_lines, LANES), f32(obs_lines, LANES)],
        [wide_scratch(n // 2), small, small],
        **half_cost,
    )
    col_own, gen, gen_sq = call(
        functools.partial(first_kernel, half),
        (core, same, other, obs, mass_gen, half_own),
        [col_out, jax.ShapeDtypeStruct((n, LANES), points_gen.dtype), f32(lines, LANES)],
        [wide_scratch(n // 2), small, small],
        **half_cost,
    )
    col_all = over_row(col_own)
    row_own, obs_add, gen_add, matrix = call(
        second_kernel,
        (obs, gen, mass_obs, col_all),
        [row_out, f32(obs_lines, LANES), f32(lines, LANES), jax.ShapeDtypeStruct((m, n), jnp.bfloat16)],
        [wide_scratch(m), gen_small, gen_small],
        **cost,
    )
    row_all = over_col(row_own)
    first = row_own
    for step in range(1, ITERS):
        (col_own,) = call(
            col_kernel,
            (matrix, obs, gen, mass_gen, row_all, first, obs_add, gen_add),
            [col_out],
            [wide_scratch(n), small, small],
            **product_cost,
        )
        col_all = over_row(col_own)
        if step == ITERS - 1:
            break
        (row_own,) = call(
            row_kernel,
            (matrix, obs, gen, mass_obs, col_all, obs_add, gen_add),
            [row_out],
            [wide_scratch(m), gen_small, gen_small],
            **product_cost,
        )
        row_all = over_col(row_own)
    potential_obs, row_lse, keep, send = call(
        mean_kernel,
        (core, matrix, obs, gen, mass_obs, col_all, obs_add, gen_add, obs_sq),
        [f32(obs_lines, LANES), f32(lines, LANES), f32(half, own, LANES), f32(half, own, LANES)],
        [wide_scratch(m), gen_small, gen_small, wide_scratch(n)],
        **product_cost,
    )
    came = lax.ppermute(send.astype(jnp.float16), "col", pair).astype(jnp.float32)
    came_lse = lax.ppermute(row_lse, "col", pair)
    (joined,) = call(
        pair_kernel, (core, keep, came, row_lse, came_lse), [f32(half, own + 2 * lines, LANES)], [wide_scratch(n)]
    )
    joined_all = over_chips(joined.astype(jnp.float16)).astype(jnp.float32)
    span = own // LANES + 1
    potential_gen, costate = call(
        last_kernel,
        (col.reshape(1), joined_all, points_gen, mass_gen, gen_sq),
        [f32(lines, LANES), f32(own, LANES)],
        [pltpu.VMEM((half, lines, LANES), jnp.float32), pltpu.VMEM((half, span * LANES, LANES), jnp.float32)],
    )
    return potential_gen.reshape(-1), potential_obs.reshape(-1), costate


def solution(mesh):
    return jax.shard_map(
        functools.partial(body, mesh.shape["row"], mesh.shape["col"]),
        mesh=mesh,
        in_specs=(P(("row", "col"), None), P(("col", "row"), None), P("row"), P("col")),
        out_specs=(P("row"), P("col"), P(("row", "col"), None)),
        check_vma=False,
    )
```

```python
import functools
import math

import jax
import jax.numpy as jnp
from jax import lax
from jax.experimental import pallas as pl
from jax.experimental.pallas import tpu as pltpu
from jax.sharding import PartitionSpec as P

ITERS = 4
LANES = 128
CHUNK = 256
SAMPLE = 128
LOW, HIGH = 1e-20, 1e30
STEEP, FAINT, NOTHING = 20.0, 60.0, 60.0
VMEM = pl.BlockSpec(memory_space=pltpu.VMEM)
SMEM = pl.BlockSpec(memory_space=pltpu.SMEM)
NT = (((1,), (1,)), ((), ()))


def lse_over(parts):
    top = functools.reduce(jnp.maximum, parts)
    return top + jnp.log(sum(jnp.exp(part - top) for part in parts))


def planes(ref):
    return [ref[k] for k in range(ref.shape[0])]


def scores(left, right, left_wide):
    prod = lax.dot_general(left, right, NT, preferred_element_type=jnp.float32)
    return prod + jnp.concatenate([left_wide] * (right.shape[0] // LANES), axis=1)


def fold(values, op):
    rows, width = values.shape
    return op(values.reshape(rows // 8, 8, width), axis=0)


def store_row(ref, first, row):
    for part in range(row.shape[1] // LANES):
        ref[pl.ds(first + part, 1), :] = row[:, part * LANES : (part + 1) * LANES]


def dense_of(row):
    return jnp.concatenate([row[:, k * LANES : (k + 1) * LANES] for k in range(row.shape[1] // LANES)], axis=0)


def row_of(dense):
    return jnp.concatenate([dense[k : k + 1, :] for k in range(dense.shape[0])], axis=1)


def widen(dense, wide_ref):
    for part in range(dense.shape[0]):
        row = jnp.broadcast_to(dense[part : part + 1, :], (LANES, LANES))
        wide_ref[part * LANES : (part + 1) * LANES, :] = jnp.transpose(row)


def squares(points):
    wide = points.astype(jnp.float32)
    square = wide * wide
    high = square.astype(jnp.bfloat16)
    low = (square - high.astype(jnp.float32)).astype(jnp.bfloat16)
    ones = jnp.ones((8, LANES), jnp.bfloat16)
    row = lax.dot_general(ones, high, NT, preferred_element_type=jnp.float32)
    row += lax.dot_general(ones, low, NT, preferred_element_type=jnp.float32)
    return dense_of(row[:1, :])


def in_parts(row):
    high = row.astype(jnp.bfloat16).astype(jnp.float32)
    middle = (row - high).astype(jnp.bfloat16).astype(jnp.float32)
    low = row - high - middle
    line = lax.broadcasted_iota(jnp.int32, (16, row.shape[1]), 0)
    parts = jnp.where(line == 0, high, jnp.where(line == 1, middle, jnp.where(line == 2, low, 0.0)))
    return parts.astype(jnp.bfloat16)


def means_of(left_ref, chunk, values, mean_ref):
    left_t = jnp.transpose(left_ref[...].astype(jnp.float32))
    left_t = jnp.concatenate([left_t, jnp.ones((16, left_t.shape[1]), jnp.float32)], axis=0).astype(jnp.bfloat16)
    numer = jnp.dot(left_t, values.astype(jnp.bfloat16), preferred_element_type=jnp.float32)
    mean = numer[:LANES, :] / numer[LANES : LANES + 1, :]
    mean_ref[pl.ds(pl.multiple_of(chunk * CHUNK, CHUNK), CHUNK), :] = jnp.transpose(mean)


def exact_pass(left_ref, right_ref, wide_ref, shift_ref, total_ref, mean_ref=None):
    n, m = left_ref.shape[0], right_ref.shape[0]
    block = 512
    per = CHUNK // LANES

    def one(chunk, carry):
        right = right_ref[pl.ds(pl.multiple_of(chunk * CHUNK, CHUNK), CHUNK), :]

        def largest(step, top):
            rows = pl.ds(pl.multiple_of(step * block, block), block)
            return jnp.maximum(top, fold(scores(left_ref[rows, :], right, wide_ref[rows, :]), jnp.max))

        top = lax.fori_loop(0, n // block, largest, jnp.full((8, CHUNK), -3e38, jnp.float32))
        top = jnp.max(top, axis=0, keepdims=True)

        def add(step, total):
            rows = pl.ds(pl.multiple_of(step * block, block), block)
            return total + fold(jnp.exp(scores(left_ref[rows, :], right, wide_ref[rows, :]) - top), jnp.sum)

        total = lax.fori_loop(0, n // block, add, jnp.zeros((8, CHUNK), jnp.float32))
        store_row(shift_ref, chunk * per, top)
        store_row(total_ref, chunk * per, jnp.sum(total, axis=0, keepdims=True))
        if mean_ref is not None:
            means_of(left_ref, chunk, jnp.exp(scores(left_ref[...], right, wide_ref[...]) - top), mean_ref)
        return carry

    lax.fori_loop(0, m // CHUNK, one, 0)


def sampled_pass(left_ref, right_ref, wide_ref, shift_ref, total_ref, matrix_ref=None):
    m = right_ref.shape[0]
    per = CHUNK // LANES
    for chunk in range(m // CHUNK):
        right = right_ref[chunk * CHUNK : (chunk + 1) * CHUNK, :]
        some = scores(left_ref[:SAMPLE, :], right, wide_ref[:SAMPLE, :])
        shift = jnp.max(fold(some, jnp.max), axis=0, keepdims=True)
        values = jnp.exp(scores(left_ref[...], right, wide_ref[...]) - shift)
        total = jnp.sum(fold(values, jnp.sum), axis=0, keepdims=True)
        store_row(shift_ref, chunk * per, shift)
        store_row(total_ref, chunk * per, total)
        if matrix_ref is not None:
            matrix_ref[:, chunk * CHUNK : (chunk + 1) * CHUNK] = values.astype(jnp.bfloat16)

    @pl.when(jnp.logical_not(jnp.max(total_ref[...]) < HIGH))
    def _():
        exact_pass(left_ref, right_ref, wide_ref, shift_ref, total_ref)
        if matrix_ref is not None:
            for chunk in range(m // CHUNK):
                across = pl.ds(chunk * CHUNK, CHUNK)
                top = row_of(shift_ref[chunk * per : (chunk + 1) * per, :])
                values = jnp.exp(scores(left_ref[...], right_ref[across, :], wide_ref[...]) - top)
                matrix_ref[:, across] = values.astype(jnp.bfloat16)

    return shift_ref[...] + jnp.log(total_ref[...])


def spread(out_ref, value):
    for copy in range(out_ref.shape[0]):
        out_ref[copy] = value


def of_core(dense, core, count):
    swapped = pltpu.roll(dense, LANES // 2, axis=1)
    left = lax.broadcasted_iota(jnp.int32, (1, LANES), 1) < LANES // 2
    halves = dense.shape[0] // count
    chosen = []
    for parity in range(2):
        sources = [(2 * k + parity) * halves + t for k in range(count) for t in range(halves)]
        rows = []
        for one, two in zip(sources[::2], sources[1::2]):
            first = (swapped if one % 2 else dense)[one // 2 : one // 2 + 1, :]
            second = (dense if two % 2 else swapped)[two // 2 : two // 2 + 1, :]
            rows.append(jnp.where(left, first, second))
        chosen.append(jnp.concatenate(rows, axis=0))
    return jnp.where(core == 0, chosen[0], chosen[1])


def fan_kernel(obs_ref, gen_ref, mass_ref, obs_out_ref, gen_out_ref, mass_out_ref):
    spread(obs_out_ref, obs_ref[...])
    spread(gen_out_ref, gen_ref[...])
    mass_out_ref[...] = mass_ref[...]


def half_kernel(count, core_ref, same_ref, right_ref, mass_ref, out_ref, right_sq_ref, wide_ref, shift_ref, total_ref):
    right_sq_ref[...] = squares(right_ref[...])
    mass = of_core(mass_ref[...], core_ref[0], count)
    widen(mass - 0.5 * squares(same_ref[...]), wide_ref)
    out_ref[...] = sampled_pass(same_ref, right_ref, wide_ref, shift_ref, total_ref)


def first_kernel(
    count, core_ref, same_ref, other_ref, right_ref, mass_ref, half_ref,
    out_ref, left_ref, wide_ref, shift_ref, total_ref,
):
    core = core_ref[0]
    own = same_ref.shape[0] // count
    for k in range(count):
        rows = pl.ds(k * own, own)
        left_ref[pl.ds(pl.multiple_of((2 * k + core) * own, 64), own), :] = same_ref[rows, :]
        left_ref[pl.ds(pl.multiple_of((2 * k + 1 - core) * own, 64), own), :] = other_ref[rows, :]
    mass = of_core(mass_ref[...], 1 - core, count)
    widen(mass - 0.5 * squares(other_ref[...]), wide_ref)
    result = sampled_pass(other_ref, right_ref, wide_ref, shift_ref, total_ref)
    spread(out_ref, lse_over([half_ref[...], result]))


def second_kernel(
    left_ref, right_ref, mass_ref, from_ref,
    out_ref, left_add_ref, right_add_ref, matrix_ref, wide_ref, shift_ref, total_ref,
):
    offset = 2.0 * mass_ref[...] - lse_over(planes(from_ref))
    left_add_ref[...] = offset
    widen(offset, wide_ref)
    spread(out_ref, sampled_pass(left_ref, right_ref, wide_ref, shift_ref, total_ref, matrix_ref))
    right_add_ref[...] = -shift_ref[...]


def close_pass(left_ref, right_ref, offset, bad, add_ref, wide_ref, shift_ref, total_ref, mean_ref=None):
    shift_ref[...] = -add_ref[...]
    totals = total_ref[...]
    fits = (totals > LOW) & (totals < HIGH)
    marks = [jnp.where(mask, 1.0, 0.0) for mask in (bad, jnp.logical_not(fits))]
    flags = [mark[k : k + 8, :] for mark in marks for k in range(0, mark.shape[0], 8)]

    @pl.when(jnp.max(functools.reduce(jnp.maximum, flags)) > 0.0)
    def _():
        widen(offset, wide_ref)
        exact_pass(left_ref, right_ref, wide_ref, shift_ref, total_ref, mean_ref)


def col_kernel(
    matrix_ref, obs_ref, gen_ref, mass_ref, from_ref, first_ref, obs_add_ref, gen_add_ref,
    out_ref, wide_ref, shift_ref, total_ref,
):
    offset = 2.0 * mass_ref[...] - lse_over(planes(from_ref))
    gain = offset - gen_add_ref[...]
    level = offset + first_ref[0]
    factors = jnp.exp(gain)
    for block in range(obs_ref.shape[0] // LANES):
        rows = pl.ds(block * LANES, LANES)
        total = jnp.zeros((LANES, LANES), jnp.float32)
        for part in range(gain.shape[0]):
            values = matrix_ref[rows, part * LANES : (part + 1) * LANES].astype(jnp.float32)
            total += values * factors[part : part + 1, :]
        total_ref[block : block + 1, :] = jnp.sum(jnp.transpose(total), axis=0, keepdims=True)
    bad = (level > STEEP) | ((gain < -FAINT) & (level > -NOTHING))
    close_pass(gen_ref, obs_ref, offset, bad, obs_add_ref, wide_ref, shift_ref, total_ref)
    spread(out_ref, shift_ref[...] + jnp.log(total_ref[...]))


def row_kernel(
    matrix_ref, obs_ref, gen_ref, mass_ref, from_ref, obs_add_ref, gen_add_ref,
    out_ref, wide_ref, shift_ref, total_ref,
):
    offset = 2.0 * mass_ref[...] - lse_over(planes(from_ref))
    gain = offset - obs_add_ref[...]
    total = jnp.dot(in_parts(row_of(jnp.exp(gain))), matrix_ref[...], preferred_element_type=jnp.float32)
    total_ref[...] = dense_of(jnp.sum(total[:8, :], axis=0, keepdims=True))
    close_pass(obs_ref, gen_ref, offset, wild(gain), gen_add_ref, wide_ref, shift_ref, total_ref)
    spread(out_ref, shift_ref[...] + jnp.log(total_ref[...]))


def wild(gain):
    return (gain > STEEP) | (gain < -FAINT)


def squares_kernel(points_ref, out_ref):
    out_ref[...] = squares(points_ref[...])


def in_halves(values):
    spaced = values * 8193.0
    high = spaced - (spaced - values)
    return high, values - high


def mean_kernel(
    core_ref, matrix_ref, left_ref, right_ref, mass_ref, from_ref, left_add_ref, right_add_ref, left_sq_ref,
    potential_ref, keep_ref, send_ref, wide_ref, shift_ref, total_ref, mean_ref,
):
    offset = 2.0 * mass_ref[...] - lse_over(planes(from_ref))
    potential_ref[...] = 2.0 * (offset - mass_ref[...]) + left_sq_ref[...]
    gain = offset - left_add_ref[...]
    weight = row_of(jnp.exp(gain))
    left_t = jnp.transpose(left_ref[...].astype(jnp.float32)) * weight
    high = left_t.astype(jnp.bfloat16)
    low = (left_t - high.astype(jnp.float32)).astype(jnp.bfloat16)
    factors = jnp.concatenate([high, low, in_parts(weight)], axis=0)
    for chunk in range(right_ref.shape[0] // CHUNK):
        across = pl.ds(chunk * CHUNK, CHUNK)
        sums = jnp.dot(factors, matrix_ref[:, across], preferred_element_type=jnp.float32)
        total = jnp.sum(sums[2 * LANES : 2 * LANES + 8, :], axis=0, keepdims=True)
        store_row(total_ref, chunk * CHUNK // LANES, total)
        mean_ref[across, :] = jnp.transpose((sums[:LANES, :] + sums[LANES : 2 * LANES, :]) / total)
    close_pass(left_ref, right_ref, offset, wild(gain), right_add_ref, wide_ref, shift_ref, total_ref, mean_ref)
    core = core_ref[0]
    count, own, _ = keep_ref.shape
    for k in range(count):
        keep_ref[k] = mean_ref[pl.ds(pl.multiple_of((2 * k + core) * own, 64), own), :]
        send_ref[k * own : (k + 1) * own, :] = mean_ref[pl.ds(pl.multiple_of((2 * k + 1 - core) * own, 64), own), :]
    lines = total_ref.shape[0]
    high, low = in_halves(shift_ref[...] + jnp.log(total_ref[...]))
    send_ref[count * own : count * own + lines, :] = high
    send_ref[count * own + lines :, :] = low


def pair_kernel(core_ref, keep_ref, came_ref, lse_ref, out_ref, wide_ref):
    core = core_ref[0]
    count, own, _ = keep_ref.shape
    lines = lse_ref.shape[0] // 2
    mine = lse_ref[:lines, :] + lse_ref[lines:, :]
    after = count * own
    both = lse_over([mine, came_ref[after : after + lines, :] + came_ref[after + lines :, :]])
    high, low = in_halves(both)
    widen(jnp.exp(mine - both), wide_ref)
    for k in range(count):
        share = wide_ref[pl.ds(pl.multiple_of((2 * k + core) * own, 64), own), :]
        came = came_ref[k * own : (k + 1) * own, :]
        out_ref[k, :own, :] = came + share * (keep_ref[k] - came)
        out_ref[k, own : own + lines, :] = high
        out_ref[k, own + lines :, :] = low


def last_kernel(col_ref, all_ref, points_ref, mass_ref, sq_ref, gen_ref, costate_ref, share_ref, wide_ref):
    own = points_ref.shape[0]
    count = all_ref.shape[0]
    lines = mass_ref.shape[0]
    parts = [all_ref[k, own : own + lines, :] + all_ref[k, own + lines :, :] for k in range(count)]
    total = lse_over(parts)
    gen_ref[...] = 2.0 * mass_ref[...] + sq_ref[...] - 2.0 * total
    first = col_ref[0] * own
    line = first // LANES
    inside = pl.multiple_of(first - line * LANES, 64)
    result = points_ref[...].astype(jnp.float32)
    span = wide_ref.shape[1] // LANES
    for k in range(count):
        share_ref[k] = jnp.exp(parts[k] - total)
        for part in range(span):
            row = jnp.broadcast_to(share_ref[k, pl.ds(line + part, 1), :], (LANES, LANES))
            wide_ref[k, part * LANES : (part + 1) * LANES, :] = jnp.transpose(row)
        result -= wide_ref[k, pl.ds(inside, own), :] * all_ref[k, :own, :]
    costate_ref[...] = result


def call(kernel, ins, outs, scratch, flops=0, exps=0, room=28):
    moved = sum(math.prod(x.shape) * x.dtype.itemsize for x in list(ins) + list(outs))
    return pl.pallas_call(
        kernel,
        out_shape=outs,
        in_specs=[SMEM if x.dtype == jnp.int32 else VMEM for x in ins],
        out_specs=[VMEM] * len(outs),
        scratch_shapes=scratch,
        compiler_params=pltpu.CompilerParams(vmem_limit_bytes=room * 2**20),
        cost_estimate=pl.CostEstimate(flops=flops, bytes_accessed=moved, transcendentals=exps),
    )(*ins)


def f32(*shape):
    return jax.ShapeDtypeStruct(shape, jnp.float32)


def wide_scratch(n):
    return pltpu.VMEM((n, LANES), jnp.float32)


def body(n_row, n_col, points_gen, points_obs, log_mass_gen, log_mass_obs):
    own = points_gen.shape[0]
    half = n_col // 2
    groups = [list(range(core, n_col, 2)) for core in range(2)]
    pair = [(k, k ^ 1) for k in range(n_col)]
    col = lax.axis_index("col").astype(jnp.int32)
    core = lax.rem(col, 2).reshape(1)
    n, m = own * n_col, points_obs.shape[0] * n_row
    lines, obs_lines = n // LANES, m // LANES

    def over_row(blocks):
        return lax.all_to_all(blocks, "row", 0, 0)

    def over_col(blocks):
        return lax.all_to_all(blocks, "col", 0, 0)

    def over_chips(blocks):
        return lax.all_to_all(blocks, "col", 0, 0, axis_index_groups=groups)

    mass_gen = log_mass_gen.reshape(lines, LANES)
    mass_obs = log_mass_obs.reshape(obs_lines, LANES)
    obs_copies, gen_copies, mass_gen = pl.pallas_call(
        fan_kernel,
        grid=(1,),
        out_shape=[
            jax.ShapeDtypeStruct((n_row,) + points_obs.shape, points_obs.dtype),
            jax.ShapeDtypeStruct((half,) + points_gen.shape, points_gen.dtype),
            f32(lines, LANES),
        ],
        in_specs=[pl.BlockSpec(x.shape, lambda step: (0, 0)) for x in (points_obs, points_gen, mass_gen)],
        out_specs=[VMEM] * 3,
        compiler_params=pltpu.CompilerParams(vmem_limit_bytes=28 * 2**20),
    )(points_obs, points_gen, mass_gen)
    obs = over_row(obs_copies).reshape(m, LANES)
    obs, gen_copies = lax.optimization_barrier((obs, gen_copies))
    same = over_chips(gen_copies)
    other = lax.ppermute(same, "col", pair)

    cost = dict(flops=2 * n * m * LANES, exps=n * m)
    product_cost = dict(flops=2 * n * m * LANES)
    small, gen_small = wide_scratch(obs_lines), wide_scratch(lines)
    col_out, row_out = f32(n_row, obs_lines, LANES), f32(n_col, lines, LANES)
    same, other = same.reshape(n // 2, LANES), other.reshape(n // 2, LANES)
    half_cost = dict(flops=n * m * LANES, exps=n * m // 2)
    half_own, obs_sq = call(
        functools.partial(half_kernel, half),
        (core, same, obs, mass_gen),
        [f32(obs_lines, LANES), f32(obs_lines, LANES)],
        [wide_scratch(n // 2), small, small],
        **half_cost,
    )
    col_own, gen = call(
        functools.partial(first_kernel, half),
        (core, same, other, obs, mass_gen, half_own),
        [col_out, jax.ShapeDtypeStruct((n, LANES), points_gen.dtype)],
        [wide_scratch(n // 2), small, small],
        **half_cost,
    )
    col_all = over_row(col_own)
    row_own, obs_add, gen_add, matrix = call(
        second_kernel,
        (obs, gen, mass_obs, col_all),
        [row_out, f32(obs_lines, LANES), f32(lines, LANES), jax.ShapeDtypeStruct((m, n), jnp.bfloat16)],
        [wide_scratch(m), gen_small, gen_small],
        **cost,
    )
    row_all = over_col(row_own)
    first = row_own
    for step in range(1, ITERS):
        (col_own,) = call(
            col_kernel,
            (matrix, obs, gen, mass_gen, row_all, first, obs_add, gen_add),
            [col_out],
            [wide_scratch(n), small, small],
            **product_cost,
        )
        col_all = over_row(col_own)
        if step == ITERS - 1:
            break
        (row_own,) = call(
            row_kernel,
            (matrix, obs, gen, mass_obs, col_all, obs_add, gen_add),
            [row_out],
            [wide_scratch(m), gen_small, gen_small],
            **product_cost,
        )
        row_all = over_col(row_own)
    potential_obs, keep, send = call(
        mean_kernel,
        (core, matrix, obs, gen, mass_obs, col_all, obs_add, gen_add, obs_sq),
        [f32(obs_lines, LANES), f32(half, own, LANES), f32(n // 2 + 2 * lines, LANES)],
        [wide_scratch(m), gen_small, gen_small, wide_scratch(n)],
        **product_cost,
    )
    send = send.astype(jnp.float16)
    came = lax.ppermute(send, "col", pair).astype(jnp.float32)
    mine = send[n // 2 :, :].astype(jnp.float32)
    gen_last, _ = lax.optimization_barrier((gen, send))
    (gen_sq,) = call(squares_kernel, (gen_last,), [f32(lines, LANES)], [])
    came, gen_sq = lax.optimization_barrier((came, gen_sq))
    (joined,) = call(
        pair_kernel, (core, keep, came, mine), [f32(half, own + 2 * lines, LANES)], [wide_scratch(n)]
    )
    joined_all = over_chips(joined.astype(jnp.float16)).astype(jnp.float32)
    span = own // LANES + 1
    potential_gen, costate = call(
        last_kernel,
        (col.reshape(1), joined_all, points_gen, mass_gen, gen_sq),
        [f32(lines, LANES), f32(own, LANES)],
        [pltpu.VMEM((half, lines, LANES), jnp.float32), pltpu.VMEM((half, span * LANES, LANES), jnp.float32)],
    )
    return potential_gen.reshape(-1), potential_obs.reshape(-1), costate


def solution(mesh):
    return jax.shard_map(
        functools.partial(body, mesh.shape["row"], mesh.shape["col"]),
        mesh=mesh,
        in_specs=(P(("row", "col"), None), P(("col", "row"), None), P("row"), P("col")),
        out_specs=(P("row"), P("col"), P(("row", "col"), None)),
        check_vma=False,
    )
```

```python
import functools
import math

import jax
import jax.numpy as jnp
from jax import lax
from jax.experimental import pallas as pl
from jax.experimental.pallas import tpu as pltpu
from jax.sharding import PartitionSpec as P

ITERS = 4
LANES = 128
CHUNK = 256
SAMPLE = 128
LOW, HIGH = 1e-20, 1e30
STEEP, FAINT, DEEP, NOTHING = 20.0, 60.0, 86.0, 60.0
VMEM = pl.BlockSpec(memory_space=pltpu.VMEM)
SMEM = pl.BlockSpec(memory_space=pltpu.SMEM)
NT = (((1,), (1,)), ((), ()))


def lse_over(parts):
    top = functools.reduce(jnp.maximum, parts)
    return top + jnp.log(sum(jnp.exp(part - top) for part in parts))


def planes(ref):
    return [ref[k] for k in range(ref.shape[0])]


def scores(left, right, left_wide):
    prod = lax.dot_general(left, right, NT, preferred_element_type=jnp.float32)
    return prod + jnp.concatenate([left_wide] * (right.shape[0] // LANES), axis=1)


def fold(values, op):
    rows, width = values.shape
    return op(values.reshape(rows // 8, 8, width), axis=0)


def store_row(ref, first, row):
    for part in range(row.shape[1] // LANES):
        ref[pl.ds(first + part, 1), :] = row[:, part * LANES : (part + 1) * LANES]


def dense_of(row):
    return jnp.concatenate([row[:, k * LANES : (k + 1) * LANES] for k in range(row.shape[1] // LANES)], axis=0)


def row_of(dense):
    return jnp.concatenate([dense[k : k + 1, :] for k in range(dense.shape[0])], axis=1)


def widen(dense, wide_ref):
    for part in range(dense.shape[0]):
        row = jnp.broadcast_to(dense[part : part + 1, :], (LANES, LANES))
        wide_ref[part * LANES : (part + 1) * LANES, :] = jnp.transpose(row)


def squares(points):
    wide = points.astype(jnp.float32)
    square = wide * wide
    high = square.astype(jnp.bfloat16)
    low = (square - high.astype(jnp.float32)).astype(jnp.bfloat16)
    ones = jnp.ones((8, LANES), jnp.bfloat16)
    row = lax.dot_general(ones, high, NT, preferred_element_type=jnp.float32)
    row += lax.dot_general(ones, low, NT, preferred_element_type=jnp.float32)
    return dense_of(row[:1, :])


def in_parts(row):
    high = row.astype(jnp.bfloat16).astype(jnp.float32)
    middle = (row - high).astype(jnp.bfloat16).astype(jnp.float32)
    low = row - high - middle
    line = lax.broadcasted_iota(jnp.int32, (16, row.shape[1]), 0)
    parts = jnp.where(line == 0, high, jnp.where(line == 1, middle, jnp.where(line == 2, low, 0.0)))
    return parts.astype(jnp.bfloat16)


def means_of(left_ref, chunk, values, mean_ref):
    left_t = jnp.transpose(left_ref[...].astype(jnp.float32))
    left_t = jnp.concatenate([left_t, jnp.ones((16, left_t.shape[1]), jnp.float32)], axis=0).astype(jnp.bfloat16)
    numer = jnp.dot(left_t, values.astype(jnp.bfloat16), preferred_element_type=jnp.float32)
    mean = numer[:LANES, :] / numer[LANES : LANES + 1, :]
    mean_ref[pl.ds(pl.multiple_of(chunk * CHUNK, CHUNK), CHUNK), :] = jnp.transpose(mean)


def exact_pass(left_ref, right_ref, wide_ref, shift_ref, total_ref, mean_ref=None):
    n, m = left_ref.shape[0], right_ref.shape[0]
    block = 512
    per = CHUNK // LANES

    def one(chunk, carry):
        right = right_ref[pl.ds(pl.multiple_of(chunk * CHUNK, CHUNK), CHUNK), :]

        def largest(step, top):
            rows = pl.ds(pl.multiple_of(step * block, block), block)
            return jnp.maximum(top, fold(scores(left_ref[rows, :], right, wide_ref[rows, :]), jnp.max))

        top = lax.fori_loop(0, n // block, largest, jnp.full((8, CHUNK), -3e38, jnp.float32))
        top = jnp.max(top, axis=0, keepdims=True)

        def add(step, total):
            rows = pl.ds(pl.multiple_of(step * block, block), block)
            return total + fold(jnp.exp(scores(left_ref[rows, :], right, wide_ref[rows, :]) - top), jnp.sum)

        total = lax.fori_loop(0, n // block, add, jnp.zeros((8, CHUNK), jnp.float32))
        store_row(shift_ref, chunk * per, top)
        store_row(total_ref, chunk * per, jnp.sum(total, axis=0, keepdims=True))
        if mean_ref is not None:
            means_of(left_ref, chunk, jnp.exp(scores(left_ref[...], right, wide_ref[...]) - top), mean_ref)
        return carry

    lax.fori_loop(0, m // CHUNK, one, 0)


def sampled_pass(left_ref, right_ref, wide_ref, shift_ref, total_ref, matrix_ref=None):
    m = right_ref.shape[0]
    per = CHUNK // LANES
    for chunk in range(m // CHUNK):
        right = right_ref[chunk * CHUNK : (chunk + 1) * CHUNK, :]
        some = scores(left_ref[:SAMPLE, :], right, wide_ref[:SAMPLE, :])
        shift = jnp.max(fold(some, jnp.max), axis=0, keepdims=True)
        values = jnp.exp(scores(left_ref[...], right, wide_ref[...]) - shift)
        total = jnp.sum(fold(values, jnp.sum), axis=0, keepdims=True)
        store_row(shift_ref, chunk * per, shift)
        store_row(total_ref, chunk * per, total)
        if matrix_ref is not None:
            matrix_ref[:, chunk * CHUNK : (chunk + 1) * CHUNK] = values.astype(jnp.bfloat16)

    @pl.when(jnp.logical_not(jnp.max(total_ref[...]) < HIGH))
    def _():
        exact_pass(left_ref, right_ref, wide_ref, shift_ref, total_ref)
        if matrix_ref is not None:
            for chunk in range(m // CHUNK):
                across = pl.ds(chunk * CHUNK, CHUNK)
                top = row_of(shift_ref[chunk * per : (chunk + 1) * per, :])
                values = jnp.exp(scores(left_ref[...], right_ref[across, :], wide_ref[...]) - top)
                matrix_ref[:, across] = values.astype(jnp.bfloat16)

    return shift_ref[...] + jnp.log(total_ref[...])


def spread(out_ref, value):
    for copy in range(out_ref.shape[0]):
        out_ref[copy] = value


def of_core(dense, core, count):
    swapped = pltpu.roll(dense, LANES // 2, axis=1)
    left = lax.broadcasted_iota(jnp.int32, (1, LANES), 1) < LANES // 2
    halves = dense.shape[0] // count
    chosen = []
    for parity in range(2):
        sources = [(2 * k + parity) * halves + t for k in range(count) for t in range(halves)]
        rows = []
        for one, two in zip(sources[::2], sources[1::2]):
            first = (swapped if one % 2 else dense)[one // 2 : one // 2 + 1, :]
            second = (dense if two % 2 else swapped)[two // 2 : two // 2 + 1, :]
            rows.append(jnp.where(left, first, second))
        chosen.append(jnp.concatenate(rows, axis=0))
    return jnp.where(core == 0, chosen[0], chosen[1])


def fan_kernel(obs_ref, gen_ref, mass_ref, obs_out_ref, gen_out_ref, mass_out_ref):
    spread(obs_out_ref, obs_ref[...])
    spread(gen_out_ref, gen_ref[...])
    mass_out_ref[...] = mass_ref[...]


def half_kernel(count, core_ref, same_ref, right_ref, mass_ref, out_ref, right_sq_ref, wide_ref, shift_ref, total_ref):
    right_sq_ref[...] = squares(right_ref[...])
    mass = of_core(mass_ref[...], core_ref[0], count)
    widen(mass - 0.5 * squares(same_ref[...]), wide_ref)
    out_ref[...] = sampled_pass(same_ref, right_ref, wide_ref, shift_ref, total_ref)


def first_kernel(
    count, core_ref, same_ref, other_ref, right_ref, mass_ref, half_ref,
    out_ref, left_ref, wide_ref, shift_ref, total_ref,
):
    core = core_ref[0]
    own = same_ref.shape[0] // count
    for k in range(count):
        rows = pl.ds(k * own, own)
        left_ref[pl.ds(pl.multiple_of((2 * k + core) * own, 64), own), :] = same_ref[rows, :]
        left_ref[pl.ds(pl.multiple_of((2 * k + 1 - core) * own, 64), own), :] = other_ref[rows, :]
    mass = of_core(mass_ref[...], 1 - core, count)
    widen(mass - 0.5 * squares(other_ref[...]), wide_ref)
    result = sampled_pass(other_ref, right_ref, wide_ref, shift_ref, total_ref)
    spread(out_ref, lse_over([half_ref[...], result]))


def second_kernel(
    left_ref, right_ref, mass_ref, from_ref,
    out_ref, left_add_ref, right_add_ref, matrix_ref, wide_ref, shift_ref, total_ref,
):
    offset = 2.0 * mass_ref[...] - lse_over(planes(from_ref))
    left_add_ref[...] = offset
    widen(offset, wide_ref)
    spread(out_ref, sampled_pass(left_ref, right_ref, wide_ref, shift_ref, total_ref, matrix_ref))
    right_add_ref[...] = -shift_ref[...]


def close_pass(left_ref, right_ref, offset, bad, add_ref, wide_ref, shift_ref, total_ref, mean_ref=None):
    shift_ref[...] = -add_ref[...]
    totals = total_ref[...]
    fits = (totals > LOW) & (totals < HIGH)
    marks = [jnp.where(mask, 1.0, 0.0) for mask in (bad, jnp.logical_not(fits))]
    flags = [mark[k : k + 8, :] for mark in marks for k in range(0, mark.shape[0], 8)]

    @pl.when(jnp.max(functools.reduce(jnp.maximum, flags)) > 0.0)
    def _():
        widen(offset, wide_ref)
        exact_pass(left_ref, right_ref, wide_ref, shift_ref, total_ref, mean_ref)


def col_kernel(
    matrix_ref, obs_ref, gen_ref, mass_ref, from_ref, first_ref, obs_add_ref, gen_add_ref,
    out_ref, wide_ref, shift_ref, total_ref,
):
    offset = 2.0 * mass_ref[...] - lse_over(planes(from_ref))
    gain = offset - gen_add_ref[...]
    level = offset + first_ref[0]
    factors = jnp.exp(gain)
    for block in range(obs_ref.shape[0] // LANES):
        rows = pl.ds(block * LANES, LANES)
        total = jnp.zeros((LANES, LANES), jnp.float32)
        for part in range(gain.shape[0]):
            values = matrix_ref[rows, part * LANES : (part + 1) * LANES].astype(jnp.float32)
            total += values * factors[part : part + 1, :]
        total_ref[block : block + 1, :] = jnp.sum(jnp.transpose(total), axis=0, keepdims=True)
    bad = (level > STEEP) | ((gain < -DEEP) & (level > -NOTHING))
    close_pass(gen_ref, obs_ref, offset, bad, obs_add_ref, wide_ref, shift_ref, total_ref)
    spread(out_ref, shift_ref[...] + jnp.log(total_ref[...]))


def row_kernel(
    matrix_ref, obs_ref, gen_ref, mass_ref, from_ref, obs_add_ref, gen_add_ref,
    out_ref, wide_ref, shift_ref, total_ref,
):
    offset = 2.0 * mass_ref[...] - lse_over(planes(from_ref))
    gain = offset - obs_add_ref[...]
    total = jnp.dot(in_parts(row_of(jnp.exp(gain))), matrix_ref[...], preferred_element_type=jnp.float32)
    total_ref[...] = dense_of(jnp.sum(total[:8, :], axis=0, keepdims=True))
    close_pass(obs_ref, gen_ref, offset, wild(gain), gen_add_ref, wide_ref, shift_ref, total_ref)
    spread(out_ref, shift_ref[...] + jnp.log(total_ref[...]))


def wild(gain):
    return (gain > STEEP) | (gain < -FAINT)


def squares_kernel(points_ref, out_ref):
    out_ref[...] = squares(points_ref[...])


def in_halves(values):
    spaced = values * 8193.0
    high = spaced - (spaced - values)
    return high, values - high


def mean_kernel(
    core_ref, matrix_ref, left_ref, right_ref, mass_ref, from_ref, left_add_ref, right_add_ref, left_sq_ref,
    potential_ref, keep_ref, send_ref, wide_ref, shift_ref, total_ref, mean_ref,
):
    offset = 2.0 * mass_ref[...] - lse_over(planes(from_ref))
    potential_ref[...] = 2.0 * (offset - mass_ref[...]) + left_sq_ref[...]
    gain = offset - left_add_ref[...]
    weight = row_of(jnp.exp(gain))
    left_t = jnp.transpose(left_ref[...].astype(jnp.float32)) * weight
    high = left_t.astype(jnp.bfloat16)
    low = (left_t - high.astype(jnp.float32)).astype(jnp.bfloat16)
    factors = jnp.concatenate([high, low, in_parts(weight)], axis=0)
    for chunk in range(right_ref.shape[0] // CHUNK):
        across = pl.ds(chunk * CHUNK, CHUNK)
        sums = jnp.dot(factors, matrix_ref[:, across], preferred_element_type=jnp.float32)
        total = jnp.sum(sums[2 * LANES : 2 * LANES + 8, :], axis=0, keepdims=True)
        store_row(total_ref, chunk * CHUNK // LANES, total)
        mean_ref[across, :] = jnp.transpose((sums[:LANES, :] + sums[LANES : 2 * LANES, :]) / total)
    close_pass(left_ref, right_ref, offset, wild(gain), right_add_ref, wide_ref, shift_ref, total_ref, mean_ref)
    core = core_ref[0]
    count, own, _ = keep_ref.shape
    for k in range(count):
        keep_ref[k] = mean_ref[pl.ds(pl.multiple_of((2 * k + core) * own, 64), own), :]
        send_ref[k * own : (k + 1) * own, :] = mean_ref[pl.ds(pl.multiple_of((2 * k + 1 - core) * own, 64), own), :]
    lines = total_ref.shape[0]
    high, low = in_halves(shift_ref[...] + jnp.log(total_ref[...]))
    send_ref[count * own : count * own + lines, :] = high
    send_ref[count * own + lines :, :] = low


def pair_kernel(core_ref, keep_ref, came_ref, lse_ref, out_ref, wide_ref):
    core = core_ref[0]
    count, own, _ = keep_ref.shape
    lines = lse_ref.shape[0] // 2
    mine = lse_ref[:lines, :] + lse_ref[lines:, :]
    after = count * own
    both = lse_over([mine, came_ref[after : after + lines, :] + came_ref[after + lines :, :]])
    high, low = in_halves(both)
    widen(jnp.exp(mine - both), wide_ref)
    for k in range(count):
        share = wide_ref[pl.ds(pl.multiple_of((2 * k + core) * own, 64), own), :]
        came = came_ref[k * own : (k + 1) * own, :]
        out_ref[k, :own, :] = came + share * (keep_ref[k] - came)
        out_ref[k, own : own + lines, :] = high
        out_ref[k, own + lines :, :] = low


def last_kernel(col_ref, all_ref, points_ref, mass_ref, sq_ref, gen_ref, costate_ref, share_ref, wide_ref):
    own = points_ref.shape[0]
    count = all_ref.shape[0]
    lines = mass_ref.shape[0]
    parts = [all_ref[k, own : own + lines, :] + all_ref[k, own + lines :, :] for k in range(count)]
    total = lse_over(parts)
    gen_ref[...] = 2.0 * mass_ref[...] + sq_ref[...] - 2.0 * total
    first = col_ref[0] * own
    line = first // LANES
    inside = pl.multiple_of(first - line * LANES, 64)
    result = points_ref[...].astype(jnp.float32)
    span = wide_ref.shape[1] // LANES
    for k in range(count):
        share_ref[k] = jnp.exp(parts[k] - total)
        for part in range(span):
            row = jnp.broadcast_to(share_ref[k, pl.ds(line + part, 1), :], (LANES, LANES))
            wide_ref[k, part * LANES : (part + 1) * LANES, :] = jnp.transpose(row)
        result -= wide_ref[k, pl.ds(inside, own), :] * all_ref[k, :own, :]
    costate_ref[...] = result


def call(kernel, ins, outs, scratch, flops=0, exps=0, room=28):
    moved = sum(math.prod(x.shape) * x.dtype.itemsize for x in list(ins) + list(outs))
    return pl.pallas_call(
        kernel,
        out_shape=outs,
        in_specs=[SMEM if x.dtype == jnp.int32 else VMEM for x in ins],
        out_specs=[VMEM] * len(outs),
        scratch_shapes=scratch,
        compiler_params=pltpu.CompilerParams(vmem_limit_bytes=room * 2**20),
        cost_estimate=pl.CostEstimate(flops=flops, bytes_accessed=moved, transcendentals=exps),
    )(*ins)


def f32(*shape):
    return jax.ShapeDtypeStruct(shape, jnp.float32)


def wide_scratch(n):
    return pltpu.VMEM((n, LANES), jnp.float32)


def body(n_row, n_col, points_gen, points_obs, log_mass_gen, log_mass_obs):
    own = points_gen.shape[0]
    half = n_col // 2
    groups = [list(range(core, n_col, 2)) for core in range(2)]
    pair = [(k, k ^ 1) for k in range(n_col)]
    col = lax.axis_index("col").astype(jnp.int32)
    core = lax.rem(col, 2).reshape(1)
    n, m = own * n_col, points_obs.shape[0] * n_row
    lines, obs_lines = n // LANES, m // LANES

    def over_row(blocks):
        return lax.all_to_all(blocks, "row", 0, 0)

    def over_col(blocks):
        return lax.all_to_all(blocks, "col", 0, 0)

    def over_chips(blocks):
        return lax.all_to_all(blocks, "col", 0, 0, axis_index_groups=groups)

    mass_gen = log_mass_gen.reshape(lines, LANES)
    mass_obs = log_mass_obs.reshape(obs_lines, LANES)
    obs_copies, gen_copies, mass_gen = pl.pallas_call(
        fan_kernel,
        grid=(1,),
        out_shape=[
            jax.ShapeDtypeStruct((n_row,) + points_obs.shape, points_obs.dtype),
            jax.ShapeDtypeStruct((half,) + points_gen.shape, points_gen.dtype),
            f32(lines, LANES),
        ],
        in_specs=[pl.BlockSpec(x.shape, lambda step: (0, 0)) for x in (points_obs, points_gen, mass_gen)],
        out_specs=[VMEM] * 3,
        compiler_params=pltpu.CompilerParams(vmem_limit_bytes=28 * 2**20),
    )(points_obs, points_gen, mass_gen)
    obs = over_row(obs_copies).reshape(m, LANES)
    obs, gen_copies = lax.optimization_barrier((obs, gen_copies))
    same = over_chips(gen_copies)
    other = lax.ppermute(same, "col", pair)

    cost = dict(flops=2 * n * m * LANES, exps=n * m)
    product_cost = dict(flops=2 * n * m * LANES)
    small, gen_small = wide_scratch(obs_lines), wide_scratch(lines)
    col_out, row_out = f32(n_row, obs_lines, LANES), f32(n_col, lines, LANES)
    same, other = same.reshape(n // 2, LANES), other.reshape(n // 2, LANES)
    half_cost = dict(flops=n * m * LANES, exps=n * m // 2)
    half_own, obs_sq = call(
        functools.partial(half_kernel, half),
        (core, same, obs, mass_gen),
        [f32(obs_lines, LANES), f32(obs_lines, LANES)],
        [wide_scratch(n // 2), small, small],
        **half_cost,
    )
    col_own, gen = call(
        functools.partial(first_kernel, half),
        (core, same, other, obs, mass_gen, half_own),
        [col_out, jax.ShapeDtypeStruct((n, LANES), points_gen.dtype)],
        [wide_scratch(n // 2), small, small],
        **half_cost,
    )
    col_all = over_row(col_own)
    row_own, obs_add, gen_add, matrix = call(
        second_kernel,
        (obs, gen, mass_obs, col_all),
        [row_out, f32(obs_lines, LANES), f32(lines, LANES), jax.ShapeDtypeStruct((m, n), jnp.bfloat16)],
        [wide_scratch(m), gen_small, gen_small],
        **cost,
    )
    row_all = over_col(row_own)
    first = row_own
    for step in range(1, ITERS):
        (col_own,) = call(
            col_kernel,
            (matrix, obs, gen, mass_gen, row_all, first, obs_add, gen_add),
            [col_out],
            [wide_scratch(n), small, small],
            **product_cost,
        )
        col_all = over_row(col_own)
        if step == ITERS - 1:
            break
        (row_own,) = call(
            row_kernel,
            (matrix, obs, gen, mass_obs, col_all, obs_add, gen_add),
            [row_out],
            [wide_scratch(m), gen_small, gen_small],
            **product_cost,
        )
        row_all = over_col(row_own)
    potential_obs, keep, send = call(
        mean_kernel,
        (core, matrix, obs, gen, mass_obs, col_all, obs_add, gen_add, obs_sq),
        [f32(obs_lines, LANES), f32(half, own, LANES), f32(n // 2 + 2 * lines, LANES)],
        [wide_scratch(m), gen_small, gen_small, wide_scratch(n)],
        **product_cost,
    )
    send = send.astype(jnp.float16)
    came = lax.ppermute(send, "col", pair).astype(jnp.float32)
    mine = send[n // 2 :, :].astype(jnp.float32)
    gen_last, _ = lax.optimization_barrier((gen, send))
    (gen_sq,) = call(squares_kernel, (gen_last,), [f32(lines, LANES)], [])
    came, gen_sq = lax.optimization_barrier((came, gen_sq))
    (joined,) = call(
        pair_kernel, (core, keep, came, mine), [f32(half, own + 2 * lines, LANES)], [wide_scratch(n)]
    )
    joined_all = over_chips(joined.astype(jnp.float16)).astype(jnp.float32)
    span = own // LANES + 1
    potential_gen, costate = call(
        last_kernel,
        (col.reshape(1), joined_all, points_gen, mass_gen, gen_sq),
        [f32(lines, LANES), f32(own, LANES)],
        [pltpu.VMEM((half, lines, LANES), jnp.float32), pltpu.VMEM((half, span * LANES, LANES), jnp.float32)],
    )
    return potential_gen.reshape(-1), potential_obs.reshape(-1), costate


def solution(mesh):
    return jax.shard_map(
        functools.partial(body, mesh.shape["row"], mesh.shape["col"]),
        mesh=mesh,
        in_specs=(P(("row", "col"), None), P(("col", "row"), None), P("row"), P("col")),
        out_specs=(P("row"), P("col"), P(("row", "col"), None)),
        check_vma=False,
    )
```
